32 devices in a mesh: atoms: 4 (over y, x), frames: 8 (over z, core).
Axes of the slice: x: 2, y: 2, z: 4, core: 2. Of those that a mesh axis runs over, the one named last changes fastest.
Arguments:
- frames: float32 [192, 3, 98304], P('frames', None, 'atoms'), may hold values from -48 to 48
- mean_structure: float32 [3, 98304], P(None, 'atoms'), may hold values from -16 to 16
- atom_weight: float32 [98304], P('atoms'), may hold values from 1 to 32
- subspace: bfloat16 [32, 3, 98304], P(None, None, 'atoms'), may hold values from -6 to 6
Outputs:
- new_mean: float32 [3, 98304], P(None, ('atoms', 'frames'))
- image: float32 [32, 3, 98304], P(None, None, ('atoms', 'frames'))
- basis: float32 [32, 3, 98304], P(None, None, ('atoms', 'frames'))
The draws below stay inside these ranges and needn't reach their ends.
All inputs are finite; a program needn't handle non-finite values.
Results may differ from the reference program's by a relative error of at most 0.0076.
Values may be sent and summed in bfloat16 or wider, within the bound.
No kernel may reach another device: no remote copies, remote signals or barrier semaphores. Data moves between devices by JAX's collectives and lax.ppermute only.
A program may use at most 128 MiB of HBM per device.

```python
import math
import jax
import jax.numpy as jnp
from jax import lax

A = 98304
K = 32
NEWTON = 8
F_DEV = 24
F = 192


def structure_parts(key):
    index = jnp.arange(A).astype(jnp.float32)
    spread = 1.0 + 2.0 * index / (A - 1)
    plane = jax.random.truncated_normal(jax.random.fold_in(key, 11), -4.0, 4.0, (2, A), jnp.float32) * spread[None, :]
    depth = jax.random.truncated_normal(jax.random.fold_in(key, 12), -4.0, 4.0, (1, A), jnp.float32) * 0.5
    offset = jnp.array([1.0, -0.5, 0.3], jnp.float32)[:, None]
    return jnp.concatenate([plane, depth], axis=0) + offset


def collective_motion(key):
    pattern = jax.random.truncated_normal(jax.random.fold_in(key, 21), -4.0, 4.0, (4, 3, A), jnp.float32) * 0.5
    amplitude = jax.random.truncated_normal(jax.random.fold_in(key, 22), -4.0, 4.0, (F, 4), jnp.float32) * 0.15
    motion = amplitude[:, 0][:, None, None] * pattern[0][None]
    for mode in range(1, 4):
        motion = motion + amplitude[:, mode][:, None, None] * pattern[mode][None]
    return motion


def draw_mean_structure(key, part):
    return structure_parts(key)


def draw_frames(key, part):
    base = structure_parts(key)
    drift = jax.random.truncated_normal(jax.random.fold_in(key, 13), -4.0, 4.0, (3, A), jnp.float32) * 0.3
    noise = jax.random.truncated_normal(jax.random.fold_in(key, 14), -4.0, 4.0, (F, 3, A), jnp.float32) * 0.5
    angles = jax.random.uniform(jax.random.fold_in(key, 15), (3, F), jnp.float32, -math.pi, math.pi)
    shift = jax.random.truncated_normal(jax.random.fold_in(key, 16), -4.0, 4.0, (3, F), jnp.float32) * 2.0
    cosa, sina = (jnp.cos(angles[0]), jnp.sin(angles[0]))
    cosb, sinb = (jnp.cos(angles[1]), jnp.sin(angles[1]))
    cosc, sinc = (jnp.cos(angles[2]), jnp.sin(angles[2]))
    rows = [[cosa * cosb, cosa * sinb * sinc - sina * cosc, cosa * sinb * cosc + sina * sinc], [sina * cosb, sina * sinb * sinc + cosa * cosc, sina * sinb * cosc - cosa * sinc], [-sinb, cosb * sinc, cosb * cosc]]
    points = base[None] + drift[None] + noise + collective_motion(key)
    result = []
    for i in range(3):
        value = rows[i][0][:, None] * points[:, 0] + rows[i][1][:, None] * points[:, 1] + rows[i][2][:, None] * points[:, 2]
        result.append(value + shift[i][:, None])
    return jnp.stack(result, axis=1)


def block_scale(stream_key, extent, pieces, low, top_value):
    factor_of, own = 1.0, jax.random.fold_in(stream_key, 6)
    for position, shards_of in pieces:
        draws = jnp.exp(jax.random.uniform(jax.random.fold_in(own, position), (shards_of,), jnp.float32, low / len(pieces), top_value / len(pieces)))
        factor_of = factor_of * jnp.repeat(draws, extent[position] // shards_of).reshape([-1 if axis == position else 1 for axis in range(len(extent))])
    return factor_of


def normal_values(own_key, dims, scale, bound, shards=(), kind=jnp.bfloat16):
    gain = block_scale(own_key, dims, shards, -0.22, 0.18) if shards else 1.0
    values = jax.random.normal(own_key, dims, jnp.float32) * scale * gain
    return jnp.minimum(jnp.maximum(values, -bound), bound).astype(kind)


def setup_inputs(seed: int = 0) -> dict:
    streams_of = jax.random.split(jax.random.key(seed), 5)
    frames = draw_frames(jax.random.fold_in(streams_of[4], 71), 0)
    mean_structure = draw_mean_structure(jax.random.fold_in(streams_of[4], 71), 0)
    atom_weight = jnp.clip(jnp.exp(math.log(32.0) - 3.465736 * jax.random.uniform(streams_of[2], (A,), jnp.float32) ** block_scale(streams_of[2], (A,), ((0, 4),), -0.2, 0.2)), 1.0, 32.0)
    subspace = normal_values(streams_of[3], (K, 3, A), 1.0, 6.0, ((2, 4),))
    return {"frames": frames, "mean_structure": mean_structure, "atom_weight": atom_weight, "subspace": subspace}


def newton_polar(moment):
    norm = jnp.sqrt(lax.optimization_barrier(jnp.sum(moment * moment, axis=(1, 2))))
    x = moment / norm[:, None, None]
    for step in range(NEWTON):
        x00, x01, x02 = (x[:, 0, 0], x[:, 0, 1], x[:, 0, 2])
        x10, x11, x12 = (x[:, 1, 0], x[:, 1, 1], x[:, 1, 2])
        x20, x21, x22 = (x[:, 2, 0], x[:, 2, 1], x[:, 2, 2])
        c00 = x11 * x22 - x12 * x21
        c01 = x12 * x20 - x10 * x22
        c02 = x10 * x21 - x11 * x20
        c10 = x02 * x21 - x01 * x22
        c11 = x00 * x22 - x02 * x20
        c12 = x01 * x20 - x00 * x21
        c20 = x01 * x12 - x02 * x11
        c21 = x02 * x10 - x00 * x12
        c22 = x00 * x11 - x01 * x10
        determ = x00 * c00 + x01 * c01 + x02 * c02
        cofac = jnp.stack([jnp.stack([c00, c01, c02], axis=1), jnp.stack([c10, c11, c12], axis=1), jnp.stack([c20, c21, c22], axis=1)], axis=1)
        x = 0.5 * (x + cofac / determ[:, None, None])
    return x

def reference(frames, mean_structure, atom_weight, subspace):
    highest = lax.Precision.HIGHEST
    total = jnp.sum(atom_weight)
    mean_center = lax.optimization_barrier(jnp.sum(atom_weight[None, :] * mean_structure, axis=1)) / total
    frame_center = jnp.einsum('a,fia->fi', atom_weight, frames, precision=highest) / total
    centered = (mean_structure - mean_center[:, None]) * atom_weight[None, :]
    moment = jnp.einsum('ia,fja->fij', centered, frames, precision=highest) / total
    rotation = newton_polar(moment)
    anchor = mean_center[:, None] - mean_structure

    def align_block(inputs):
        block, rot, center = inputs
        moved = jnp.einsum('fij,fja->fia', rot, block, precision=highest)
        offset = jnp.einsum('fij,fj->fi', rot, center, precision=highest)
        return (moved - offset[:, :, None] + anchor[None]).astype(jnp.bfloat16)
    blocks = F // F_DEV
    displaced = lax.map(align_block, (frames.reshape(blocks, F_DEV, 3, A), rotation.reshape(blocks, F_DEV, 3, 3), frame_center.reshape(blocks, F_DEV, 3)))
    displaced = displaced.reshape(F, 3 * A)
    new_mean = mean_structure + lax.optimization_barrier(jnp.sum(displaced, axis=0, dtype=jnp.float32)).reshape(3, A) / F
    projection = jnp.dot(displaced.astype(jnp.float32), subspace.reshape(K, 3 * A).T.astype(jnp.float32), preferred_element_type=jnp.float32)
    centered_projection = (projection - lax.optimization_barrier(jnp.sum(projection, axis=0)) / F).astype(jnp.bfloat16)
    flat = jnp.dot(centered_projection.T.astype(jnp.float32), displaced.astype(jnp.float32), preferred_element_type=jnp.float32) / F
    gram = jnp.dot(flat, flat.T, precision=highest) / (3 * A)
    lower = jnp.linalg.cholesky(gram)
    basis = jax.scipy.linalg.solve_triangular(lower, flat, lower=True)
    return (new_mean, flat.reshape(K, 3, A), basis.reshape(K, 3, A))
```

```python
import functools

import jax
import jax.numpy as jnp
from jax import lax
from jax.experimental import pallas as pl
from jax.experimental.pallas import tpu as pltpu
from jax.sharding import PartitionSpec as P

NEWTON = 8
LANES = 128
F32 = jnp.float32
BF16 = jnp.bfloat16
TILE = 256
PANEL = 4
VMEM_LIMIT = 24 * 1024 * 1024


def params():
    return pltpu.CompilerParams(vmem_limit_bytes=VMEM_LIMIT)


def in_vmem(count):
    return [pl.BlockSpec(memory_space=pltpu.VMEM)] * count


def split3(value):
    high = value.astype(BF16)
    rest = value - high.astype(F32)
    middle = rest.astype(BF16)
    low = (rest - middle.astype(F32)).astype(BF16)
    return high, middle, low


def dot_nt(a, b):
    return lax.dot_general(a, b, (((1,), (1,)), ((), ())), preferred_element_type=F32)


def dot_nn(a, b, precision=None):
    return lax.dot_general(
        a, b, (((1,), (0,)), ((), ())), preferred_element_type=F32, precision=precision
    )


def moments_kernel(
    _, x_hbm, m_hbm, w_hbm, s_hbm, out_ref, x_ref, m_ref, w_ref, lhs_ref, rhs_ref, sems
):
    rows, atoms = x_ref.shape
    vectors = s_hbm.shape[0]
    chunks = sems.shape[1] - 1
    chunk = atoms // chunks
    n = rows + 8
    copies = [
        [
            pltpu.make_async_copy(m_hbm, m_ref, sems.at[0, chunks]),
            pltpu.make_async_copy(w_hbm, w_ref, sems.at[1, chunks]),
        ]
    ]
    for t in range(chunks):
        lanes = pl.ds(t * chunk, chunk)
        copies.append(
            [
                pltpu.make_async_copy(x_hbm.at[:, lanes], x_ref.at[:, lanes], sems.at[0, t]),
                pltpu.make_async_copy(
                    s_hbm.at[:, lanes], rhs_ref.at[0:vectors, lanes], sems.at[1, t]
                ),
            ]
        )
    for group in copies:
        for copy in group:
            copy.start()
    for copy in copies[0]:
        copy.wait()
    row = lax.broadcasted_iota(jnp.int32, (8, TILE), 0)
    ones = jnp.where(row == 3, 1.0, 0.0)
    total = jnp.zeros(out_ref.shape, F32)
    for t in range(chunks):
        for copy in copies[t + 1]:
            copy.wait()
        for start in range(0, chunk, TILE):
            lanes = slice(t * chunk + start, t * chunk + start + TILE)
            here = slice(start, start + TILE)
            left = ones
            for i in range(3):
                left = jnp.where(row == i, m_ref[i : i + 1, lanes], left)
            value = jnp.concatenate([x_ref[:, lanes], left], axis=0)
            high = value.astype(BF16)
            lhs_ref[t % 2, 0:n, here] = high
            lhs_ref[t % 2, n : 2 * n, here] = (value - high.astype(F32)).astype(BF16)
            pieces = [v.astype(F32) for v in split3(left * w_ref[:, lanes])]
            aux = jnp.concatenate(pieces + [jnp.zeros(left.shape, F32)], axis=0)
            rhs_ref[vectors:, lanes] = aux.astype(BF16)
        sums = dot_nt(lhs_ref[t % 2], rhs_ref[:, t * chunk : (t + 1) * chunk])
        total = total + (sums[0:n] + sums[n : 2 * n])
    out_ref[...] = total


def moments(where_, x, mean, weight, sub):
    rows, atoms = x.shape
    vectors = sub.shape[0]
    chunks = 16
    chunk = atoms // chunks
    n = rows + 8
    return pl.pallas_call(
        moments_kernel,
        in_specs=[pl.BlockSpec(memory_space=pltpu.SMEM)] + [pl.BlockSpec(memory_space=pl.ANY)] * 4,
        out_specs=in_vmem(2),
        out_shape=(jax.ShapeDtypeStruct((n, LANES), F32), jax.ShapeDtypeStruct(x.shape, F32)),
        scratch_shapes=[
            pltpu.VMEM(mean.shape, F32),
            pltpu.VMEM(weight.shape, F32),
            pltpu.VMEM((2, 2 * n, chunk), BF16),
            pltpu.VMEM((LANES, atoms), BF16),
            pltpu.SemaphoreType.DMA((2, chunks + 1)),
        ],
        compiler_params=params(),
        name="moments",
    )(where_, x, mean, weight, sub)


def rotate_kernel(frame_rows, vectors, *refs):
    parts, (coef_ref, proj_ref) = refs[:-2], refs[-2:]
    sums = parts[0][...]
    for ref in parts[1:]:
        sums = sums + ref[...]
    folded = sums + pltpu.roll(sums, LANES - 8, 1) + pltpu.roll(sums, LANES - 16, 1)
    base = 3 * vectors
    tail = 3 * frame_rows
    shape = (frame_rows, LANES)
    lane = lax.broadcasted_iota(jnp.int32, shape, 1)

    def scalar(r, c):
        return jnp.broadcast_to(folded[r : r + 1, c : c + 1], shape)

    def column(j, c):
        return jnp.broadcast_to(folded[j * frame_rows : (j + 1) * frame_rows, c : c + 1], shape)

    total = scalar(tail + 3, base + 3)
    center = [scalar(tail + 3, base + i) / total for i in range(3)]
    frame_center = [column(j, base + 3) / total for j in range(3)]
    x = [
        [column(j, base + i) / total - center[i] * frame_center[j] for j in range(3)]
        for i in range(3)
    ]
    square = sum(x[i][j] * x[i][j] for i in range(3) for j in range(3))
    norm = jnp.sqrt(square)
    x = [[x[i][j] / norm for j in range(3)] for i in range(3)]
    for _ in range(NEWTON):
        cof = [
            [
                x[(i + 1) % 3][(j + 1) % 3] * x[(i + 2) % 3][(j + 2) % 3]
                - x[(i + 1) % 3][(j + 2) % 3] * x[(i + 2) % 3][(j + 1) % 3]
                for j in range(3)
            ]
            for i in range(3)
        ]
        determ = x[0][0] * cof[0][0] + x[0][1] * cof[0][1] + x[0][2] * cof[0][2]
        inverse = 1.0 / determ
        x = [[0.5 * (x[i][j] + cof[i][j] * inverse) for j in range(3)] for i in range(3)]
    shift = [
        center[i] - (x[i][0] * frame_center[0] + x[i][1] * frame_center[1] + x[i][2] * frame_center[2])
        for i in range(3)
    ]
    for i in range(3):
        for j in range(3):
            at = (3 * i + j) * frame_rows
            coef_ref[at : at + frame_rows, :] = x[i][j]
        at = (9 + i) * frame_rows
        coef_ref[at : at + frame_rows, :] = shift[i]

    def by_group(values):
        return jnp.where(lane < vectors, values[0], jnp.where(lane < 2 * vectors, values[1], values[2]))

    y = by_group(shift) * sums[tail + 3 : tail + 4, :]
    y = y - by_group([sums[tail + i : tail + i + 1, :] for i in range(3)])
    for j in range(3):
        block = sums[j * frame_rows : (j + 1) * frame_rows, :]
        y = y + by_group([x[i][j] for i in range(3)]) * block
    y = y + pltpu.roll(y, LANES - vectors, 1) + pltpu.roll(y, LANES - 2 * vectors, 1)
    y = jnp.where(lane < vectors, y, 0.0)
    proj_ref[...] = y


def rotate(parts, frame_rows, vectors):
    return pl.pallas_call(
        functools.partial(rotate_kernel, frame_rows, vectors),
        out_shape=(
            jax.ShapeDtypeStruct((12 * frame_rows, LANES), F32),
            jax.ShapeDtypeStruct((frame_rows, LANES), F32),
        ),
        compiler_params=params(),
        name="rotate",
    )(*parts)


def first_block(chip, line):
    end = jnp.logical_or(chip == 0, chip == line - 1)
    return jnp.where(end, line - 1 - chip, chip)


def displace_kernel(keep, first, line, frame_rows, width, idx, x_ref, m_ref, coef_ref, out_ref):
    core = lax.rem(idx[0], 2)
    side = core if keep else 1 - core
    made_first = first_block(idx[0] // 2, line)

    def coef(i):
        return coef_ref[i * frame_rows : (i + 1) * frame_rows, :]

    def do_block(b, _):
        block = made_first if first else b + (b >= made_first).astype(jnp.int32)
        for start in range(0, width, LANES):
            lanes = pl.ds(pl.multiple_of((2 * block + side) * width + start, LANES), LANES)
            x = [x_ref[j * frame_rows : (j + 1) * frame_rows, lanes] for j in range(3)]
            result = []
            for i in range(3):
                value = coef(3 * i) * x[0] + coef(3 * i + 1) * x[1] + coef(3 * i + 2) * x[2]
                result.append(value + (coef(9 + i) - m_ref[i : i + 1, lanes]))
            to = pl.ds(pl.multiple_of(b * width + start, LANES), LANES)
            out_ref[:, to] = jnp.concatenate(result, axis=0).astype(BF16)
        return 0

    lax.fori_loop(0, 1 if first else line - 1, do_block, 0)


def displace(where_, x, mean, coef, line, keep, first):
    rows, atoms = x.shape
    width = atoms // (2 * line)
    out_width = width if first else (line - 1) * width
    return pl.pallas_call(
        functools.partial(displace_kernel, keep, first, line, rows // 3, width),
        in_specs=[pl.BlockSpec(memory_space=pltpu.SMEM)] + in_vmem(3),
        out_specs=pl.BlockSpec(memory_space=pltpu.VMEM),
        out_shape=jax.ShapeDtypeStruct((rows, out_width), BF16),
        compiler_params=params(),
        name="displace",
    )(where_, x, mean, coef)


def weights_kernel(frame_rows, vectors, own_ref, other_ref, c_ref, e_ref, mean_ref):
    total = jnp.sum(own_ref[...] + other_ref[...], axis=0, keepdims=True)
    mean = total / (2 * frame_rows)
    lane = lax.broadcasted_iota(jnp.int32, (frame_rows, LANES), 1)
    for source, out in ((own_ref, c_ref), (other_ref, e_ref)):
        value = jnp.where(lane < vectors, source[...] - mean, 0.0)
        blocks = [value, pltpu.roll(value, vectors, 1), pltpu.roll(value, 2 * vectors, 1)]
        blocks.append(jnp.zeros((LANES - 3 * frame_rows, LANES), F32))
        table = jnp.concatenate(blocks, axis=0).T
        out[...] = table[0 : 3 * vectors, 0 : 3 * frame_rows].astype(BF16)
    mean_ref[...] = jnp.broadcast_to(jnp.where(lane[0:1] < vectors, mean, 0.0), (8, LANES))


def weights(own, other, frame_rows, vectors):
    out = jax.ShapeDtypeStruct((3 * vectors, 3 * frame_rows), BF16)
    return pl.pallas_call(
        functools.partial(weights_kernel, frame_rows, vectors),
        in_specs=in_vmem(2),
        out_specs=in_vmem(3),
        out_shape=(out, out, jax.ShapeDtypeStruct((8, LANES), F32)),
        compiler_params=params(),
        name="weights",
    )(own, other)


def ones_rows(rows):
    row = lax.broadcasted_iota(jnp.int32, (8, rows), 0)
    column = lax.broadcasted_iota(jnp.int32, (8, rows), 1)
    inside = jnp.logical_and(column >= row * (rows // 3), column < (row + 1) * (rows // 3))
    return jnp.where(inside, 1.0, 0.0).astype(BF16)


def both(left, right, a, b):
    return dot_nn(left, a) + dot_nn(right, b)


def as_column(row, vectors):
    return jnp.broadcast_to(row, (LANES, LANES)).T[0:vectors, 0:1]


def read_slab(slab, width):
    at = 3 * width // LANES
    center = jnp.sum(slab[at : at + 3], axis=0, keepdims=True)
    total = jnp.sum(slab[at + 3 : at + 6], axis=0, keepdims=True)
    return center, total


def write_slab(slab_ref, received, sums, center, total, width):
    tiles = width // LANES
    slab_ref[...] = received
    for i in range(3):
        for tile in range(tiles):
            at = i * tiles + tile
            part = sums[i : i + 1, tile * LANES : (tile + 1) * LANES]
            slab_ref[at : at + 1, :] = received[at : at + 1, :] + part
    for i, piece in enumerate([*split3(center), *split3(total)]):
        at = 3 * tiles + i
        slab_ref[at : at + 1, :] = piece.astype(F32)


def term_kernel(block, starts, line, p, pieces, vectors, width, idx, *refs):
    (c_ref, e_ref, mean_ref, a_ref, b_ref), refs = refs[0:5], list(refs[5:])
    slab_ref = refs.pop() if p == 0 else None
    out_ref = refs.pop()
    chip = idx[0] // 2
    if block is None:
        at = 0
    else:
        at = block(chip)
        at = jnp.clip(at - (at > first_block(chip, line)).astype(jnp.int32), 0, line - 2)
    piece_width = width // pieces
    lanes = pl.ds(pl.multiple_of(at * width + p * piece_width, LANES), piece_width)
    value = both(c_ref[...], e_ref[...], a_ref[:, lanes], b_ref[:, lanes])
    mean = mean_ref[0:1, :]
    center, total = mean, mean
    slab = jnp.zeros((value.shape[0], LANES), F32)
    ones = ones_rows(a_ref.shape[0])
    if refs:
        slab = refs[0][:, piece_width:].astype(F32)
        before, summed_means = read_slab(slab, width)
        center = jnp.where(chip == starts, mean, before)
        total = mean + summed_means
        column = as_column(mean - center, vectors)
        sums = both(ones, ones, a_ref[:, lanes], b_ref[:, lanes])
        moved = [column * sums[i : i + 1, :] for i in range(3)]
        value = value + jnp.concatenate(moved, axis=0)
        value = value + refs[p][:, 0:piece_width].astype(F32)
    out_ref[:, 0:piece_width] = value.astype(BF16)
    if p == 0:
        lanes = pl.ds(pl.multiple_of(at * width, LANES), width)
        sums = both(ones, ones, a_ref[:, lanes], b_ref[:, lanes])
        write_slab(slab_ref, slab, sums, center, total, width)
        out_ref[:, piece_width:] = slab_ref[...].astype(BF16)


def term(where_, scales, displaced, received, block, starts, line, p, pieces, vectors, width):
    rows = scales[0].shape[0]
    args = (*scales, *displaced, *received)
    out_width = width // pieces + (LANES if p == 0 else 0)
    return pl.pallas_call(
        functools.partial(term_kernel, block, starts, line, p, pieces, vectors, width),
        in_specs=[pl.BlockSpec(memory_space=pltpu.SMEM)] + in_vmem(len(args)),
        out_specs=pl.BlockSpec(memory_space=pltpu.VMEM),
        out_shape=jax.ShapeDtypeStruct((rows, out_width), BF16),
        scratch_shapes=[pltpu.VMEM((rows, LANES), F32)] if p == 0 else [],
        compiler_params=params(),
        name="term",
    )(where_, *args)


def image_kernel(line, p, pieces, vectors, width, frame_count, idx, *refs):
    refs = list(refs)
    c_ref, e_ref, mean_ref = [refs.pop(0) for _ in range(3)]
    firsts, rests = [[refs.pop(0) for _ in range(2)] for _ in range(2)]
    carriers = [refs.pop(0) for _ in range(2)]
    other_ref = refs.pop(0)
    block_ref = refs.pop()
    new_mean_ref = refs.pop() if p == 0 else None
    gram_ref, image_ref = refs.pop(), refs.pop()
    received = carriers if p == 0 else refs
    chip = idx[0] // 2
    made_first = first_block(chip, line)
    at = pl.multiple_of(jnp.clip(chip - (chip > made_first).astype(jnp.int32), 0, line - 2) * width, LANES)
    for n in range(2):

        @pl.when(chip == made_first)
        def _(n=n):
            block_ref[n] = firsts[n][...]

        @pl.when(chip != made_first)
        def _(n=n):
            block_ref[n] = rests[n][:, pl.ds(at, width)]

    piece_width = width // pieces
    lanes = slice(p * piece_width, (p + 1) * piece_width)
    value = both(c_ref[...], e_ref[...], block_ref[0, :, lanes], block_ref[1, :, lanes])
    for ref in received:
        value = value + ref[:, 0:piece_width].astype(F32)

    ones = ones_rows(block_ref.shape[1])
    sums = both(ones, ones, block_ref[0], block_ref[1])
    mean = mean_ref[0:1, :]
    slabs = [ref[:, piece_width:].astype(F32) for ref in carriers]
    centers, totals = zip(*(read_slab(slab, width) for slab in slabs))
    center = (mean + totals[0] + totals[1]) / line
    columns = [as_column(v - center, vectors) for v in (mean, *centers)]
    tiles, piece_tiles = width // LANES, piece_width // LANES
    gram = jnp.zeros((2 * vectors, LANES), F32)
    for i in range(3):
        rows = slice(i * vectors, (i + 1) * vectors)
        moved = []
        for tile in range(p * piece_tiles, (p + 1) * piece_tiles):
            part = columns[0] * sums[i : i + 1, tile * LANES : (tile + 1) * LANES]
            row = i * tiles + tile
            for column, slab in zip(columns[1:], slabs):
                part = part + column * slab[row : row + 1, :]
            moved.append(part)
        part = (value[rows] + jnp.concatenate(moved, axis=1)) / frame_count
        image_ref[rows, :] = part
        high = part.astype(BF16)
        low = (part - high.astype(F32)).astype(BF16)
        lhs = jnp.concatenate([high, low], axis=0)
        rhs = jnp.concatenate([lhs, jnp.zeros((LANES - 2 * vectors, piece_width), BF16)], axis=0)
        gram = gram + dot_nt(lhs, rhs)
    gram = gram[0:vectors] + gram[vectors : 2 * vectors]
    gram = gram + pltpu.roll(gram, LANES - vectors, 1)
    lane = lax.broadcasted_iota(jnp.int32, gram.shape, 1)
    gram = jnp.where(lane < vectors, gram, 0.0)
    packed = gram[0:8]
    for g in range(1, vectors // 8):
        packed = packed + pltpu.roll(gram[8 * g : 8 * g + 8], vectors * g, 1)
    if p > 0:
        packed = packed + other_ref[...]
    gram_ref[...] = packed
    if p == 0:
        total = slabs[0] + slabs[1]
        for i in range(3):
            for tile in range(tiles):
                start = (idx[0] * tiles + tile) * LANES
                old = other_ref[i : i + 1, pl.ds(pl.multiple_of(start, LANES), LANES)]
                row = i * tiles + tile
                here = slice(tile * LANES, (tile + 1) * LANES)
                added = (total[row : row + 1, :] + sums[i : i + 1, here]) / frame_count
                new_mean_ref[i : i + 1, here] = old + added


def image_piece(
    where_, scales, firsts, rests, carriers, received, other, line, p, pieces, vectors, width,
    frame_count,
):
    rows = scales[0].shape[0]
    args = [*scales, *firsts, *rests, *carriers, other]
    out_shape = [
        jax.ShapeDtypeStruct((rows, width // pieces), F32),
        jax.ShapeDtypeStruct((8, LANES), F32),
    ]
    if p == 0:
        out_shape.append(jax.ShapeDtypeStruct((3, width), F32))
    else:
        args += received
    return pl.pallas_call(
        functools.partial(image_kernel, line, p, pieces, vectors, width, frame_count),
        in_specs=[pl.BlockSpec(memory_space=pltpu.SMEM)] + in_vmem(len(args)),
        out_specs=in_vmem(len(out_shape)),
        out_shape=out_shape,
        scratch_shapes=[pltpu.VMEM((2, firsts[0].shape[0], width), BF16)],
        compiler_params=params(),
        name="image_piece",
    )(where_, *args)


def fold_kernel(*refs):
    value = refs[0][...]
    for ref in refs[1:-1]:
        value = value + ref[...]
    refs[-1][...] = value


def fold(parts):
    return pl.pallas_call(
        fold_kernel,
        in_specs=in_vmem(len(parts)),
        out_specs=pl.BlockSpec(memory_space=pltpu.VMEM),
        out_shape=jax.ShapeDtypeStruct(parts[0].shape, F32),
        compiler_params=params(),
        name="fold",
    )(*parts)


def exchanged(value, axis, size, bits):
    masks = [0]
    for bit in bits:
        masks += [mask | (1 << bit) for mask in masks]
    return [value] + [
        lax.ppermute(value, axis, [(i, i ^ mask) for i in range(size)]) for mask in masks[:0:-1]
    ]


def summed(value, axis, size, bits):
    groups = [bits[start : start + 2] for start in range(0, len(bits), 2)]
    for group in groups[:-1]:
        value = fold(exchanged(value, axis, size, group))
    return exchanged(value, axis, size, groups[-1])


def basis_kernel(vectors, coordinates, gram_count, *refs):
    grams, pieces, (image_ref, basis_ref) = refs[:gram_count], refs[gram_count:-2], refs[-2:]
    packed = grams[0][...]
    for ref in grams[1:]:
        packed = packed + ref[...]
    packed = packed / coordinates
    groups = [packed]
    for g in range(1, vectors // 8):
        groups.append(pltpu.roll(packed, LANES - vectors * g, 1))
    gram = jnp.concatenate(groups, axis=0)
    row = lax.broadcasted_iota(jnp.int32, gram.shape, 0)
    lane = lax.broadcasted_iota(jnp.int32, gram.shape, 1)
    a = jnp.where(lane < vectors, gram, jnp.where(lane == row + vectors, 1.0, 0.0))
    for panel in range(0, vectors, PANEL):
        columns = [
            jnp.broadcast_to(a[:, j : j + 1], a.shape) for j in range(panel, panel + PANEL)
        ]
        for q in range(PANEL):
            j = panel + q
            factor = columns[q] * (1.0 / columns[q][j : j + 1, :])
            factor = jnp.where(row > j, factor, 0.0)
            for r in range(q + 1, PANEL):
                columns[r] = columns[r] - factor * columns[r][j : j + 1, :]
            a = a - factor * a[j : j + 1, :]
    diagonal = jnp.sum(jnp.where(lane == row, a, 0.0), axis=1, keepdims=True)
    a = a * (1.0 / jnp.sqrt(diagonal))
    a = jnp.where(lane < vectors, pltpu.roll(a, LANES - vectors, 1), 0.0)
    high = a.astype(BF16).astype(F32)
    left = high + pltpu.roll(high, vectors, 1) + pltpu.roll(a - high, 2 * vectors, 1)
    left = left.astype(BF16)[:, 0 : 3 * vectors]
    start = 0
    for ref in pieces:
        lanes = slice(start, start + ref.shape[1])
        start += ref.shape[1]
        for i in range(3):
            rows = slice(i * vectors, (i + 1) * vectors)
            part = ref[rows, :]
            high = part.astype(BF16)
            low = (part - high.astype(F32)).astype(BF16)
            basis_ref[rows, lanes] = dot_nn(left, jnp.concatenate([high, low, high], axis=0))
            image_ref[rows, lanes] = part


def basis_of(grams, images, vectors, coordinates):
    rows = images[0].shape[0]
    width = sum(v.shape[1] for v in images)
    return pl.pallas_call(
        functools.partial(basis_kernel, vectors, coordinates, len(grams)),
        in_specs=in_vmem(len(grams) + len(images)),
        out_specs=in_vmem(2),
        out_shape=[jax.ShapeDtypeStruct((rows, width), F32)] * 2,
        compiler_params=params(),
        name="basis",
    )(*grams, *images)


def along_line(line, pieces, make_first, make):
    def to_right(z):
        return [(2 * z + core, 2 * z + 2 + core) for core in range(2)]

    def to_left(z):
        return [(2 * z + core, 2 * z - 2 + core) for core in range(2)]

    ends = to_right(0) + to_left(line - 1)
    right = [lax.ppermute(make_first(p), "frames", ends) for p in range(pieces)]
    left = list(right)
    for step in range(2, line):

        def right_block(chip, step=step):
            return jnp.minimum(line - step + chip, line - 1)

        def left_block(chip, step=step):
            return jnp.maximum(step - line + chip, 0)

        right_pairs = [pair for z in range(step) for pair in to_right(z)]
        left_pairs = [pair for z in range(step) for pair in to_left(line - 1 - z)]
        next_right, next_left = [], []
        for p in range(pieces):
            out = make(right[: p + 1], right_block, 0, p)
            next_right.append(lax.ppermute(out, "frames", right_pairs))
            out = make(left[: p + 1], left_block, line - 1, p)
            next_left.append(lax.ppermute(out, "frames", left_pairs))
        right, left = next_right, next_left
    return right, left


def per_device(atom_devices, frame_devices, frames, mean_structure, atom_weight, subspace):
    frame_rows, _, atoms = frames.shape
    vectors = subspace.shape[0]
    frame_count = frame_rows * frame_devices
    width = atoms // frame_devices
    line = frame_devices // 2
    pieces = 2 if (width // LANES) % 2 == 0 else 1
    assert line > 2 and 3 * width // LANES + 6 <= 3 * vectors

    x = jnp.transpose(frames, (1, 0, 2)).reshape(3 * frame_rows, atoms)
    sub = jnp.transpose(subspace, (1, 0, 2)).reshape(3 * vectors, atoms)
    where_ = lax.axis_index("frames").astype(jnp.int32).reshape(1)

    inputs = (x, mean_structure, atom_weight.reshape(1, atoms), sub)
    local, x = moments(where_, *(pltpu.with_memory_space_constraint(v, pltpu.HBM) for v in inputs))
    atom_bits = range(atom_devices.bit_length() - 1)
    coef, proj = rotate(summed(local, "atoms", atom_devices, atom_bits), frame_rows, vectors)

    swap = [(i, i ^ 1) for i in range(frame_devices)]
    proj_other = lax.ppermute(proj, "frames", swap)

    def made(keep, first, after):
        late = lax.optimization_barrier((coef, after))[0]
        return displace(where_, x, mean_structure, late, line, keep, first)

    first_sent = made(False, True, proj)
    first_own = made(True, True, first_sent)
    firsts = (first_own, lax.ppermute(first_sent, "frames", swap))
    rest_sent = made(False, False, (proj_other, first_own))
    rest_sent = lax.optimization_barrier((rest_sent, firsts[1]))[0]
    rest_other = lax.ppermute(rest_sent, "frames", swap)
    scales = weights(proj, proj_other, frame_rows, vectors)

    def make_first(p):
        nonlocal last
        last = term(where_, scales, firsts, (), None, 0, line, p, pieces, vectors, width)
        return last

    def make(received, block, starts, p):
        return term(
            where_, scales, rests(), received, block, starts, line, p, pieces, vectors, width
        )

    last, kept = None, []

    def rests():
        if not kept:
            kept.append(made(True, False, last))
        return kept[0], rest_other

    right, left = along_line(line, pieces, make_first, make)
    carriers = (right[0], left[0])
    images, gram = [], None
    for p in range(pieces):
        image, gram, *more = image_piece(
            where_, scales, firsts, rests(), carriers, (right[p], left[p]),
            mean_structure if p == 0 else gram, line, p, pieces, vectors, width, frame_count,
        )
        images.append(image)
        if p == 0:
            (new_mean,) = more
    gram = fold(summed(gram, "atoms", atom_devices, atom_bits))
    gram = fold(exchanged(gram, "frames", frame_devices, [0]))
    grams = summed(gram, "frames", frame_devices, range(1, frame_devices.bit_length() - 1))
    image, basis = basis_of(grams, images, vectors, 3 * atoms * atom_devices)

    def placed(value):
        return jnp.transpose(value.reshape(3, vectors, width), (1, 0, 2))

    return new_mean, placed(image), placed(basis)


def solution(mesh):
    return jax.shard_map(
        functools.partial(per_device, mesh.shape["atoms"], mesh.shape["frames"]),
        mesh=mesh,
        in_specs=(P("frames", None, "atoms"), P(None, "atoms"), P("atoms"), P(None, None, "atoms")),
        out_specs=(
            P(None, ("atoms", "frames")),
            P(None, None, ("atoms", "frames")),
            P(None, None, ("atoms", "frames")),
        ),
        check_vma=False,
    )
```

```python
import functools

import jax
import jax.numpy as jnp
from jax import lax
from jax.experimental import pallas as pl
from jax.experimental.pallas import tpu as pltpu
from jax.sharding import PartitionSpec as P

NEWTON = 8
LANES = 128
F32 = jnp.float32
BF16 = jnp.bfloat16
TILE = 256
PANEL = 4
VMEM_LIMIT = 24 * 1024 * 1024


def params():
    return pltpu.CompilerParams(vmem_limit_bytes=VMEM_LIMIT)


def cost(weight):
    return pl.CostEstimate(flops=weight * 10**9, bytes_accessed=1, transcendentals=0)


def in_vmem(count):
    return [pl.BlockSpec(memory_space=pltpu.VMEM)] * count


def split3(value):
    high = value.astype(BF16)
    rest = value - high.astype(F32)
    middle = rest.astype(BF16)
    low = (rest - middle.astype(F32)).astype(BF16)
    return high, middle, low


def dot_nt(a, b):
    return lax.dot_general(a, b, (((1,), (1,)), ((), ())), preferred_element_type=F32)


def dot_nn(a, b, precision=None):
    return lax.dot_general(
        a, b, (((1,), (0,)), ((), ())), preferred_element_type=F32, precision=precision
    )


def moments_kernel(
    _, x_hbm, m_hbm, w_hbm, s_hbm, out_ref, x_ref, m_ref, w_ref, lhs_ref, rhs_ref, sems
):
    rows, atoms = x_ref.shape
    vectors = s_hbm.shape[0]
    chunks = sems.shape[1] - 1
    chunk = atoms // chunks
    n = rows + 8
    copies = [
        [
            pltpu.make_async_copy(m_hbm, m_ref, sems.at[0, chunks]),
            pltpu.make_async_copy(w_hbm, w_ref, sems.at[1, chunks]),
        ]
    ]
    for t in range(chunks):
        lanes = pl.ds(t * chunk, chunk)
        copies.append(
            [
                pltpu.make_async_copy(x_hbm.at[:, lanes], x_ref.at[:, lanes], sems.at[0, t]),
                pltpu.make_async_copy(
                    s_hbm.at[:, lanes], rhs_ref.at[0:vectors, lanes], sems.at[1, t]
                ),
            ]
        )
    for group in copies:
        for copy in group:
            copy.start()
    for copy in copies[0]:
        copy.wait()
    row = lax.broadcasted_iota(jnp.int32, (8, TILE), 0)
    ones = jnp.where(row == 3, 1.0, 0.0)
    total = jnp.zeros(out_ref.shape, F32)
    for t in range(chunks):
        for copy in copies[t + 1]:
            copy.wait()
        for start in range(0, chunk, TILE):
            lanes = slice(t * chunk + start, t * chunk + start + TILE)
            here = slice(start, start + TILE)
            left = ones
            for i in range(3):
                left = jnp.where(row == i, m_ref[i : i + 1, lanes], left)
            value = jnp.concatenate([x_ref[:, lanes], left], axis=0)
            high = value.astype(BF16)
            lhs_ref[t % 2, 0:n, here] = high
            lhs_ref[t % 2, n : 2 * n, here] = (value - high.astype(F32)).astype(BF16)
            pieces = [v.astype(F32) for v in split3(left * w_ref[:, lanes])]
            aux = jnp.concatenate(pieces + [jnp.zeros(left.shape, F32)], axis=0)
            rhs_ref[vectors:, lanes] = aux.astype(BF16)
        sums = dot_nt(lhs_ref[t % 2], rhs_ref[:, t * chunk : (t + 1) * chunk])
        total = total + (sums[0:n] + sums[n : 2 * n])
    out_ref[...] = total


def moments(where_, x, mean, weight, sub):
    rows, atoms = x.shape
    vectors = sub.shape[0]
    chunks = 16
    chunk = atoms // chunks
    n = rows + 8
    return pl.pallas_call(
        moments_kernel,
        in_specs=[pl.BlockSpec(memory_space=pltpu.SMEM)] + [pl.BlockSpec(memory_space=pl.ANY)] * 4,
        out_specs=in_vmem(2),
        out_shape=(jax.ShapeDtypeStruct((n, LANES), F32), jax.ShapeDtypeStruct(x.shape, F32)),
        scratch_shapes=[
            pltpu.VMEM(mean.shape, F32),
            pltpu.VMEM(weight.shape, F32),
            pltpu.VMEM((2, 2 * n, chunk), BF16),
            pltpu.VMEM((LANES, atoms), BF16),
            pltpu.SemaphoreType.DMA((2, chunks + 1)),
        ],
        compiler_params=params(),
        name="moments",
    )(where_, x, mean, weight, sub)


def rotate_kernel(frame_rows, vectors, *refs):
    parts, (coef_ref, proj_ref) = refs[:-2], refs[-2:]
    sums = parts[0][...]
    for ref in parts[1:]:
        sums = sums + ref[...]
    folded = sums + pltpu.roll(sums, LANES - 8, 1) + pltpu.roll(sums, LANES - 16, 1)
    base = 3 * vectors
    tail = 3 * frame_rows
    shape = (frame_rows, LANES)
    lane = lax.broadcasted_iota(jnp.int32, shape, 1)

    def scalar(r, c):
        return jnp.broadcast_to(folded[r : r + 1, c : c + 1], shape)

    def column(j, c):
        return jnp.broadcast_to(folded[j * frame_rows : (j + 1) * frame_rows, c : c + 1], shape)

    total = scalar(tail + 3, base + 3)
    center = [scalar(tail + 3, base + i) / total for i in range(3)]
    frame_center = [column(j, base + 3) / total for j in range(3)]
    x = [
        [column(j, base + i) / total - center[i] * frame_center[j] for j in range(3)]
        for i in range(3)
    ]
    square = sum(x[i][j] * x[i][j] for i in range(3) for j in range(3))
    norm = jnp.sqrt(square)
    x = [[x[i][j] / norm for j in range(3)] for i in range(3)]
    for _ in range(NEWTON):
        cof = [
            [
                x[(i + 1) % 3][(j + 1) % 3] * x[(i + 2) % 3][(j + 2) % 3]
                - x[(i + 1) % 3][(j + 2) % 3] * x[(i + 2) % 3][(j + 1) % 3]
                for j in range(3)
            ]
            for i in range(3)
        ]
        determ = x[0][0] * cof[0][0] + x[0][1] * cof[0][1] + x[0][2] * cof[0][2]
        inverse = 1.0 / determ
        x = [[0.5 * (x[i][j] + cof[i][j] * inverse) for j in range(3)] for i in range(3)]
    shift = [
        center[i] - (x[i][0] * frame_center[0] + x[i][1] * frame_center[1] + x[i][2] * frame_center[2])
        for i in range(3)
    ]
    for i in range(3):
        for j in range(3):
            at = (3 * i + j) * frame_rows
            coef_ref[at : at + frame_rows, :] = x[i][j]
        at = (9 + i) * frame_rows
        coef_ref[at : at + frame_rows, :] = shift[i]

    def by_group(values):
        return jnp.where(lane < vectors, values[0], jnp.where(lane < 2 * vectors, values[1], values[2]))

    y = by_group(shift) * sums[tail + 3 : tail + 4, :]
    y = y - by_group([sums[tail + i : tail + i + 1, :] for i in range(3)])
    for j in range(3):
        block = sums[j * frame_rows : (j + 1) * frame_rows, :]
        y = y + by_group([x[i][j] for i in range(3)]) * block
    y = y + pltpu.roll(y, LANES - vectors, 1) + pltpu.roll(y, LANES - 2 * vectors, 1)
    y = jnp.where(lane < vectors, y, 0.0)
    proj_ref[...] = y


def rotate(parts, frame_rows, vectors):
    return pl.pallas_call(
        functools.partial(rotate_kernel, frame_rows, vectors),
        out_shape=(
            jax.ShapeDtypeStruct((12 * frame_rows, LANES), F32),
            jax.ShapeDtypeStruct((frame_rows, LANES), F32),
        ),
        compiler_params=params(),
        name="rotate",
    )(*parts)


def first_block(chip, line):
    end = jnp.logical_or(chip == 0, chip == line - 1)
    return jnp.where(end, line - 1 - chip, chip)


def displace_kernel(keep, first, line, frame_rows, width, idx, x_ref, m_ref, coef_ref, out_ref):
    core = lax.rem(idx[0], 2)
    side = core if keep else 1 - core
    made_first = first_block(idx[0] // 2, line)

    def coef(i):
        return coef_ref[i * frame_rows : (i + 1) * frame_rows, :]

    def do_block(b, _):
        block = made_first if first else b + (b >= made_first).astype(jnp.int32)
        for start in range(0, width, LANES):
            lanes = pl.ds(pl.multiple_of((2 * block + side) * width + start, LANES), LANES)
            x = [x_ref[j * frame_rows : (j + 1) * frame_rows, lanes] for j in range(3)]
            result = []
            for i in range(3):
                value = coef(3 * i) * x[0] + coef(3 * i + 1) * x[1] + coef(3 * i + 2) * x[2]
                result.append(value + (coef(9 + i) - m_ref[i : i + 1, lanes]))
            to = pl.ds(pl.multiple_of(b * width + start, LANES), LANES)
            out_ref[:, to] = jnp.concatenate(result, axis=0).astype(BF16)
        return 0

    lax.fori_loop(0, 1 if first else line - 1, do_block, 0)


def displace(where_, x, mean, coef, line, keep, first):
    rows, atoms = x.shape
    width = atoms // (2 * line)
    out_width = width if first else (line - 1) * width
    return pl.pallas_call(
        functools.partial(displace_kernel, keep, first, line, rows // 3, width),
        in_specs=[pl.BlockSpec(memory_space=pltpu.SMEM)] + in_vmem(3),
        out_specs=pl.BlockSpec(memory_space=pltpu.VMEM),
        out_shape=jax.ShapeDtypeStruct((rows, out_width), BF16),
        compiler_params=params(),
        name="displace",
    )(where_, x, mean, coef)


def weights_kernel(frame_rows, vectors, own_ref, other_ref, c_ref, e_ref, mean_ref):
    total = jnp.sum(own_ref[...] + other_ref[...], axis=0, keepdims=True)
    mean = total / (2 * frame_rows)
    lane = lax.broadcasted_iota(jnp.int32, (frame_rows, LANES), 1)
    for source, out in ((own_ref, c_ref), (other_ref, e_ref)):
        value = jnp.where(lane < vectors, source[...] - mean, 0.0)
        blocks = [value, pltpu.roll(value, vectors, 1), pltpu.roll(value, 2 * vectors, 1)]
        blocks.append(jnp.zeros((LANES - 3 * frame_rows, LANES), F32))
        table = jnp.concatenate(blocks, axis=0).T
        out[...] = table[0 : 3 * vectors, 0 : 3 * frame_rows].astype(BF16)
    mean_ref[...] = jnp.broadcast_to(jnp.where(lane[0:1] < vectors, mean, 0.0), (8, LANES))


def weights(own, other, frame_rows, vectors):
    out = jax.ShapeDtypeStruct((3 * vectors, 3 * frame_rows), BF16)
    return pl.pallas_call(
        functools.partial(weights_kernel, frame_rows, vectors),
        in_specs=in_vmem(2),
        out_specs=in_vmem(3),
        out_shape=(out, out, jax.ShapeDtypeStruct((8, LANES), F32)),
        compiler_params=params(),
        name="weights",
    )(own, other)


def ones_rows(rows):
    row = lax.broadcasted_iota(jnp.int32, (8, rows), 0)
    column = lax.broadcasted_iota(jnp.int32, (8, rows), 1)
    inside = jnp.logical_and(column >= row * (rows // 3), column < (row + 1) * (rows // 3))
    return jnp.where(inside, 1.0, 0.0).astype(BF16)


def both(left, right, a, b):
    return dot_nn(left, a) + dot_nn(right, b)


def as_column(row, vectors):
    return jnp.broadcast_to(row, (LANES, LANES)).T[0:vectors, 0:1]


def read_slab(slab, width):
    at = 3 * width // LANES
    center = jnp.sum(slab[at : at + 3], axis=0, keepdims=True)
    total = jnp.sum(slab[at + 3 : at + 6], axis=0, keepdims=True)
    return center, total


def write_slab(slab_ref, received, sums, center, total, width):
    tiles = width // LANES
    slab_ref[...] = received
    for i in range(3):
        for tile in range(tiles):
            at = i * tiles + tile
            part = sums[i : i + 1, tile * LANES : (tile + 1) * LANES]
            slab_ref[at : at + 1, :] = received[at : at + 1, :] + part
    for i, piece in enumerate([*split3(center), *split3(total)]):
        at = 3 * tiles + i
        slab_ref[at : at + 1, :] = piece.astype(F32)


def term_kernel(block, starts, line, p, spans, vectors, width, idx, *refs):
    (c_ref, e_ref, mean_ref, a_ref, b_ref), refs = refs[0:5], list(refs[5:])
    slab_ref = refs.pop() if p == 0 else None
    out_ref = refs.pop()
    chip = idx[0] // 2
    if block is None:
        at = 0
    else:
        at = block(chip)
        at = jnp.clip(at - (at > first_block(chip, line)).astype(jnp.int32), 0, line - 2)
    offset, piece_width = spans[p]
    lanes = pl.ds(pl.multiple_of(at * width + offset, LANES), piece_width)
    value = both(c_ref[...], e_ref[...], a_ref[:, lanes], b_ref[:, lanes])
    mean = mean_ref[0:1, :]
    center, total = mean, mean
    slab = jnp.zeros((value.shape[0], LANES), F32)
    ones = ones_rows(a_ref.shape[0])
    if refs:
        slab = refs[0][:, spans[0][1] :].astype(F32)
        center, summed_means = read_slab(slab, width)
        center = jnp.where(starts(chip), mean, center)
        total = mean + summed_means
        column = as_column(mean - center, vectors)
        sums = both(ones, ones, a_ref[:, lanes], b_ref[:, lanes])
        moved = [column * sums[i : i + 1, :] for i in range(3)]
        value = value + jnp.concatenate(moved, axis=0)
        value = value + refs[p][:, 0:piece_width].astype(F32)
    out_ref[:, 0:piece_width] = value.astype(BF16)
    if p == 0:
        lanes = pl.ds(pl.multiple_of(at * width, LANES), width)
        sums = both(ones, ones, a_ref[:, lanes], b_ref[:, lanes])
        write_slab(slab_ref, slab, sums, center, total, width)
        out_ref[:, piece_width:] = slab_ref[...].astype(BF16)


def term(where_, scales, displaced, received, block, starts, line, p, spans, vectors, width):
    rows = scales[0].shape[0]
    args = (*scales, *displaced, *received)
    out_width = spans[p][1] + (LANES if p == 0 else 0)
    return pl.pallas_call(
        functools.partial(term_kernel, block, starts, line, p, spans, vectors, width),
        in_specs=[pl.BlockSpec(memory_space=pltpu.SMEM)] + in_vmem(len(args)),
        out_specs=pl.BlockSpec(memory_space=pltpu.VMEM),
        out_shape=jax.ShapeDtypeStruct((rows, out_width), BF16),
        scratch_shapes=[pltpu.VMEM((rows, LANES), F32)] if p == 0 else [],
        compiler_params=params(),
        cost_estimate=cost(1),
        name="term",
    )(where_, *args)


def image_kernel(carrier_count, line, p, spans, vectors, width, frame_count, idx, *refs):
    refs = list(refs)
    c_ref, e_ref, mean_ref = [refs.pop(0) for _ in range(3)]
    firsts, rests = [[refs.pop(0) for _ in range(2)] for _ in range(2)]
    carriers = [refs.pop(0) for _ in range(carrier_count)]
    other_ref = refs.pop(0)
    block_ref = refs.pop()
    new_mean_ref = refs.pop() if p == 0 else None
    gram_ref, image_ref = refs.pop(), refs.pop()
    received = carriers if p == 0 else refs
    chip = idx[0] // 2
    made_first = first_block(chip, line)
    at = pl.multiple_of(jnp.clip(chip - (chip > made_first).astype(jnp.int32), 0, line - 2) * width, LANES)
    for n in range(2):

        @pl.when(chip == made_first)
        def _(n=n):
            block_ref[n] = firsts[n][...]

        @pl.when(chip != made_first)
        def _(n=n):
            block_ref[n] = rests[n][:, pl.ds(at, width)]

    offset, piece_width = spans[p]
    lanes = slice(offset, offset + piece_width)
    value = both(c_ref[...], e_ref[...], block_ref[0, :, lanes], block_ref[1, :, lanes])
    for ref in received:
        value = value + ref[:, 0:piece_width].astype(F32)

    ones = ones_rows(block_ref.shape[1])
    sums = both(ones, ones, block_ref[0], block_ref[1])
    mean = mean_ref[0:1, :]
    slabs = [ref[:, spans[0][1] :].astype(F32) for ref in carriers]
    centers, totals = zip(*(read_slab(slab, width) for slab in slabs))
    center = functools.reduce(jnp.add, totals, mean) / line
    columns = [as_column(v - center, vectors) for v in (mean, *centers)]
    tiles = width // LANES
    gram = jnp.zeros((2 * vectors, LANES), F32)
    for i in range(3):
        rows = slice(i * vectors, (i + 1) * vectors)
        moved = []
        for tile in range(offset // LANES, (offset + piece_width) // LANES):
            part = columns[0] * sums[i : i + 1, tile * LANES : (tile + 1) * LANES]
            row = i * tiles + tile
            for column, slab in zip(columns[1:], slabs):
                part = part + column * slab[row : row + 1, :]
            moved.append(part)
        part = (value[rows] + jnp.concatenate(moved, axis=1)) / frame_count
        image_ref[rows, :] = part
        high = part.astype(BF16)
        low = (part - high.astype(F32)).astype(BF16)
        lhs = jnp.concatenate([high, low], axis=0)
        rhs = jnp.concatenate([lhs, jnp.zeros((LANES - 2 * vectors, piece_width), BF16)], axis=0)
        gram = gram + dot_nt(lhs, rhs)
    gram = gram[0:vectors] + gram[vectors : 2 * vectors]
    gram = gram + pltpu.roll(gram, LANES - vectors, 1)
    lane = lax.broadcasted_iota(jnp.int32, gram.shape, 1)
    gram = jnp.where(lane < vectors, gram, 0.0)
    packed = gram[0:8]
    for g in range(1, vectors // 8):
        packed = packed + pltpu.roll(gram[8 * g : 8 * g + 8], vectors * g, 1)
    if p > 0:
        packed = packed + other_ref[...]
    gram_ref[...] = packed
    if p == 0:
        total = functools.reduce(jnp.add, slabs)
        for i in range(3):
            for tile in range(tiles):
                start = (idx[0] * tiles + tile) * LANES
                old = other_ref[i : i + 1, pl.ds(pl.multiple_of(start, LANES), LANES)]
                row = i * tiles + tile
                here = slice(tile * LANES, (tile + 1) * LANES)
                added = (total[row : row + 1, :] + sums[i : i + 1, here]) / frame_count
                new_mean_ref[i : i + 1, here] = old + added


def image_piece(
    where_, scales, firsts, rests, carriers, received, other, line, p, spans, vectors, width,
    frame_count,
):
    rows = scales[0].shape[0]
    args = [*scales, *firsts, *rests, *carriers, other]
    out_shape = [
        jax.ShapeDtypeStruct((rows, spans[p][1]), F32),
        jax.ShapeDtypeStruct((8, LANES), F32),
    ]
    if p == 0:
        out_shape.append(jax.ShapeDtypeStruct((3, width), F32))
    else:
        args += received
    return pl.pallas_call(
        functools.partial(
            image_kernel, len(carriers), line, p, spans, vectors, width, frame_count
        ),
        in_specs=[pl.BlockSpec(memory_space=pltpu.SMEM)] + in_vmem(len(args)),
        out_specs=in_vmem(len(out_shape)),
        out_shape=out_shape,
        scratch_shapes=[pltpu.VMEM((2, firsts[0].shape[0], width), BF16)],
        compiler_params=params(),
        cost_estimate=cost(2),
        name="image_piece",
    )(where_, *args)


def fold_kernel(*refs):
    value = refs[0][...]
    for ref in refs[1:-1]:
        value = value + ref[...]
    refs[-1][...] = value


def fold(parts):
    return pl.pallas_call(
        fold_kernel,
        in_specs=in_vmem(len(parts)),
        out_specs=pl.BlockSpec(memory_space=pltpu.VMEM),
        out_shape=jax.ShapeDtypeStruct(parts[0].shape, F32),
        compiler_params=params(),
        name="fold",
    )(*parts)


def exchanged(value, axis, size, bits):
    masks = [0]
    for bit in bits:
        masks += [mask | (1 << bit) for mask in masks]
    return [value] + [
        lax.ppermute(value, axis, [(i, i ^ mask) for i in range(size)]) for mask in masks[:0:-1]
    ]


def summed(value, axis, size, bits):
    groups = [bits[start : start + 2] for start in range(0, len(bits), 2)]
    for group in groups[:-1]:
        value = fold(exchanged(value, axis, size, group))
    return exchanged(value, axis, size, groups[-1])


def basis_kernel(vectors, coordinates, gram_count, *refs):
    grams, pieces = refs[:gram_count], refs[gram_count:-4]
    image_hbm, basis_hbm, basis_ref, sems = refs[-4:]
    copies, starts = [], [0]
    for n, ref in enumerate(pieces):
        starts.append(starts[n] + ref.shape[1])
        lanes = pl.ds(starts[n], ref.shape[1])
        copies.append(pltpu.make_async_copy(ref, image_hbm.at[:, lanes], sems.at[n, 3]))
        copies[-1].start()
    packed = grams[0][...]
    for ref in grams[1:]:
        packed = packed + ref[...]
    packed = packed / coordinates
    groups = [packed]
    for g in range(1, vectors // 8):
        groups.append(pltpu.roll(packed, LANES - vectors * g, 1))
    gram = jnp.concatenate(groups, axis=0)
    row = lax.broadcasted_iota(jnp.int32, gram.shape, 0)
    lane = lax.broadcasted_iota(jnp.int32, gram.shape, 1)
    a = jnp.where(lane < vectors, gram, jnp.where(lane == row + vectors, 1.0, 0.0))
    for panel in range(0, vectors, PANEL):
        columns = [
            jnp.broadcast_to(a[:, j : j + 1], a.shape) for j in range(panel, panel + PANEL)
        ]
        for q in range(PANEL):
            j = panel + q
            factor = columns[q] * (1.0 / columns[q][j : j + 1, :])
            factor = jnp.where(row > j, factor, 0.0)
            for r in range(q + 1, PANEL):
                columns[r] = columns[r] - factor * columns[r][j : j + 1, :]
            a = a - factor * a[j : j + 1, :]
    diagonal = jnp.sum(jnp.where(lane == row, a, 0.0), axis=1, keepdims=True)
    a = a * (1.0 / jnp.sqrt(diagonal))
    a = jnp.where(lane < vectors, pltpu.roll(a, LANES - vectors, 1), 0.0)
    high = a.astype(BF16).astype(F32)
    left = high + pltpu.roll(high, vectors, 1) + pltpu.roll(a - high, 2 * vectors, 1)
    left = left.astype(BF16)[:, 0 : 3 * vectors]
    for n, ref in enumerate(pieces):
        for i in range(3):
            rows, lanes = pl.ds(i * vectors, vectors), pl.ds(starts[n], ref.shape[1])
            part = ref[rows, :]
            high = part.astype(BF16)
            low = (part - high.astype(F32)).astype(BF16)
            basis_ref[rows, lanes] = dot_nn(left, jnp.concatenate([high, low, high], axis=0))
            copies.append(
                pltpu.make_async_copy(
                    basis_ref.at[rows, lanes], basis_hbm.at[rows, lanes], sems.at[n, i]
                )
            )
            copies[-1].start()
    for copy in copies:
        copy.wait()


def basis_of(grams, images, vectors, coordinates):
    rows = images[0].shape[0]
    width = sum(v.shape[1] for v in images)
    return pl.pallas_call(
        functools.partial(basis_kernel, vectors, coordinates, len(grams)),
        in_specs=in_vmem(len(grams) + len(images)),
        out_specs=[pl.BlockSpec(memory_space=pl.ANY)] * 2,
        out_shape=[jax.ShapeDtypeStruct((rows, width), F32)] * 2,
        scratch_shapes=[
            pltpu.VMEM((rows, width), F32),
            pltpu.SemaphoreType.DMA((len(images), 4)),
        ],
        compiler_params=params(),
        name="basis",
    )(*grams, *images)


def to_right(z):
    return [(2 * z + core, 2 * z + 2 + core) for core in range(2)]


def to_left(z):
    return [(2 * z + core, 2 * z - 2 + core) for core in range(2)]


def along_four(pieces, make_first, make):
    inward, middle, outward = (to_right(z) + to_left(3 - z) for z in range(3))

    def at_end(chip):
        return jnp.logical_or(chip == 0, chip == 3)

    def never(chip):
        return chip < 0

    def choose(*blocks):
        def block(chip):
            return sum(jnp.where(chip == z, d, 0) for z, d in enumerate(blocks))

        return block

    each = range(pieces)
    first = [lax.ppermute(make_first(p), "frames", inward) for p in each]
    ends, middles = [], []
    for p in each:
        out = make((), choose(2, 0, 0, 1), None, p, first[p])
        ends.append(lax.ppermute(out, "frames", inward))
        out = make(first[: p + 1], choose(0, 3, 0, 0), never, p)
        middles.append(lax.ppermute(out, "frames", middle))
    arrived = []
    for p in each:
        out = make(middles[: p + 1], choose(1, 0, 3, 2), at_end, p, ends[p])
        end = lax.ppermute(out, "frames", inward + outward)
        out = make(ends[: p + 1], choose(0, 2, 1, 0), never, p, out)
        arrived.append([end, lax.ppermute(out, "frames", middle)])
    return arrived


def along_line(line, pieces, make_first, make):
    ends = to_right(0) + to_left(line - 1)
    right = [lax.ppermute(make_first(p), "frames", ends) for p in range(pieces)]
    left = list(right)
    for step in range(2, line):

        def right_block(chip, step=step):
            return jnp.minimum(line - step + chip, line - 1)

        def left_block(chip, step=step):
            return jnp.maximum(step - line + chip, 0)

        right_pairs = [pair for z in range(step) for pair in to_right(z)]
        left_pairs = [pair for z in range(step) for pair in to_left(line - 1 - z)]
        next_right, next_left = [], []
        for p in range(pieces):
            out = make(right[: p + 1], right_block, lambda chip: chip == 0, p)
            next_right.append(lax.ppermute(out, "frames", right_pairs))
            out = make(left[: p + 1], left_block, lambda chip: chip == line - 1, p)
            next_left.append(lax.ppermute(out, "frames", left_pairs))
        right, left = next_right, next_left
    return [[right[p], left[p]] for p in range(pieces)]


def per_device(atom_devices, frame_devices, frames, mean_structure, atom_weight, subspace):
    frame_rows, _, atoms = frames.shape
    vectors = subspace.shape[0]
    frame_count = frame_rows * frame_devices
    width = atoms // frame_devices
    line = frame_devices // 2
    tiles = width // LANES
    assert line > 2 and tiles > 1 and 3 * tiles + 6 <= 3 * vectors
    cut = tiles // 2 * LANES
    spans = ((0, cut), (cut, width - cut))

    x = jnp.transpose(frames, (1, 0, 2)).reshape(3 * frame_rows, atoms)
    sub = jnp.transpose(subspace, (1, 0, 2)).reshape(3 * vectors, atoms)
    where_ = lax.axis_index("frames").astype(jnp.int32).reshape(1)

    inputs = (x, mean_structure, atom_weight.reshape(1, atoms), sub)
    local, x = moments(where_, *(pltpu.with_memory_space_constraint(v, pltpu.HBM) for v in inputs))
    atom_bits = range(atom_devices.bit_length() - 1)
    coef, proj = rotate(summed(local, "atoms", atom_devices, atom_bits), frame_rows, vectors)

    swap = [(i, i ^ 1) for i in range(frame_devices)]
    proj_other = lax.ppermute(proj, "frames", swap)

    def made(keep, first, after):
        late = lax.optimization_barrier((coef, after))[0]
        return displace(where_, x, mean_structure, late, line, keep, first)

    first_sent = made(False, True, proj)
    first_own = made(True, True, first_sent)
    firsts = (first_own, lax.ppermute(first_sent, "frames", swap))
    rest_sent = made(False, False, first_own)
    rest_sent = lax.optimization_barrier((rest_sent, firsts[1], proj_other))[0]
    rest_other = lax.ppermute(rest_sent, "frames", swap)
    scales = weights(proj, proj_other, frame_rows, vectors)

    last, kept = None, []

    def make_first(p):
        nonlocal last
        last = term(where_, scales, firsts, (), None, None, line, p, spans, vectors, width)
        return last

    def rests():
        if not kept:
            kept.append(made(True, False, last))
        return kept[0], rest_other

    def make(received, block, starts, p, after=None):
        late = scales
        if after is not None:
            late = lax.optimization_barrier((scales, after))[0]
        return term(where_, late, rests(), received, block, starts, line, p, spans, vectors, width)

    if line == 4:
        arrived = along_four(len(spans), make_first, make)
    else:
        arrived = along_line(line, len(spans), make_first, make)
    images, gram = [], None
    for p in range(len(spans)):
        image, gram, *more = image_piece(
            where_, scales, firsts, rests(), arrived[0], arrived[p],
            mean_structure if p == 0 else gram, line, p, spans, vectors, width, frame_count,
        )
        images.append(image)
        if p == 0:
            (new_mean,) = more
    gram = fold(summed(gram, "atoms", atom_devices, atom_bits))
    gram = fold(exchanged(gram, "frames", frame_devices, [0]))
    grams = summed(gram, "frames", frame_devices, range(1, frame_devices.bit_length() - 1))
    image, basis = basis_of(grams, images, vectors, 3 * atoms * atom_devices)

    def placed(value):
        return jnp.transpose(value.reshape(3, vectors, width), (1, 0, 2))

    return new_mean, placed(image), placed(basis)


def solution(mesh):
    return jax.shard_map(
        functools.partial(per_device, mesh.shape["atoms"], mesh.shape["frames"]),
        mesh=mesh,
        in_specs=(P("frames", None, "atoms"), P(None, "atoms"), P("atoms"), P(None, None, "atoms")),
        out_specs=(
            P(None, ("atoms", "frames")),
            P(None, None, ("atoms", "frames")),
            P(None, None, ("atoms", "frames")),
        ),
        check_vma=False,
    )
```

```python
import functools

import jax
import jax.numpy as jnp
from jax import lax
from jax.experimental import pallas as pl
from jax.experimental.pallas import tpu as pltpu
from jax.sharding import PartitionSpec as P

NEWTON = 8
LANES = 128
F32 = jnp.float32
BF16 = jnp.bfloat16
TILE = 256
PANEL = 4
VMEM_LIMIT = 24 * 1024 * 1024


def params():
    return pltpu.CompilerParams(vmem_limit_bytes=VMEM_LIMIT)


def cost(weight):
    return pl.CostEstimate(flops=weight * 10**9, bytes_accessed=1, transcendentals=0)


def in_vmem(count):
    return [pl.BlockSpec(memory_space=pltpu.VMEM)] * count


def split3(value):
    high = value.astype(BF16)
    rest = value - high.astype(F32)
    middle = rest.astype(BF16)
    low = (rest - middle.astype(F32)).astype(BF16)
    return high, middle, low


def dot_nt(a, b):
    return lax.dot_general(a, b, (((1,), (1,)), ((), ())), preferred_element_type=F32)


def dot_nn(a, b, precision=None):
    return lax.dot_general(
        a, b, (((1,), (0,)), ((), ())), preferred_element_type=F32, precision=precision
    )


def moments_kernel(
    _, x_hbm, m_hbm, w_hbm, s_hbm, out_ref, x_ref, m_ref, w_ref, lhs_ref, rhs_ref, sems
):
    rows, atoms = x_ref.shape
    vectors = s_hbm.shape[0]
    chunks = sems.shape[1] - 1
    chunk = atoms // chunks
    n = rows + 8
    copies = [
        [
            pltpu.make_async_copy(m_hbm, m_ref, sems.at[0, chunks]),
            pltpu.make_async_copy(w_hbm, w_ref, sems.at[1, chunks]),
        ]
    ]
    for t in range(chunks):
        lanes = pl.ds(t * chunk, chunk)
        copies.append(
            [
                pltpu.make_async_copy(x_hbm.at[:, lanes], x_ref.at[:, lanes], sems.at[0, t]),
                pltpu.make_async_copy(
                    s_hbm.at[:, lanes], rhs_ref.at[0:vectors, lanes], sems.at[1, t]
                ),
            ]
        )
    for group in copies:
        for copy in group:
            copy.start()
    for copy in copies[0]:
        copy.wait()
    row = lax.broadcasted_iota(jnp.int32, (8, TILE), 0)
    ones = jnp.where(row == 3, 1.0, 0.0)
    total = jnp.zeros(out_ref.shape, F32)

    def product(t):
        sums = dot_nt(lhs_ref[t % 2], rhs_ref[:, t * chunk : (t + 1) * chunk])
        return sums[0:n] + sums[n : 2 * n]

    for t in range(chunks):
        for copy in copies[t + 1]:
            copy.wait()
        for start in range(0, chunk, TILE):
            lanes = slice(t * chunk + start, t * chunk + start + TILE)
            here = slice(start, start + TILE)
            left = ones
            for i in range(3):
                left = jnp.where(row == i, m_ref[i : i + 1, lanes], left)
            value = jnp.concatenate([x_ref[:, lanes], left], axis=0)
            high = value.astype(BF16)
            lhs_ref[t % 2, 0:n, here] = high
            lhs_ref[t % 2, n : 2 * n, here] = (value - high.astype(F32)).astype(BF16)
            pieces = [v.astype(F32) for v in split3(left * w_ref[:, lanes])]
            aux = jnp.concatenate(pieces + [jnp.zeros(left.shape, F32)], axis=0)
            rhs_ref[vectors:, lanes] = aux.astype(BF16)
        if t > 0:
            total = total + product(t - 1)
    total = total + product(chunks - 1)
    out_ref[...] = total


def moments(where_, x, mean, weight, sub):
    rows, atoms = x.shape
    vectors = sub.shape[0]
    chunks = 16
    chunk = atoms // chunks
    n = rows + 8
    return pl.pallas_call(
        moments_kernel,
        in_specs=[pl.BlockSpec(memory_space=pltpu.SMEM)] + [pl.BlockSpec(memory_space=pl.ANY)] * 4,
        out_specs=in_vmem(2),
        out_shape=(jax.ShapeDtypeStruct((n, LANES), F32), jax.ShapeDtypeStruct(x.shape, F32)),
        scratch_shapes=[
            pltpu.VMEM(mean.shape, F32),
            pltpu.VMEM(weight.shape, F32),
            pltpu.VMEM((2, 2 * n, chunk), BF16),
            pltpu.VMEM((LANES, atoms), BF16),
            pltpu.SemaphoreType.DMA((2, chunks + 1)),
        ],
        compiler_params=params(),
        name="moments",
    )(where_, x, mean, weight, sub)


def rotate_kernel(frame_rows, vectors, *refs):
    parts, (coef_ref, proj_ref) = refs[:-2], refs[-2:]
    sums = parts[0][...]
    for ref in parts[1:]:
        sums = sums + ref[...]
    folded = sums + pltpu.roll(sums, LANES - 8, 1) + pltpu.roll(sums, LANES - 16, 1)
    base = 3 * vectors
    tail = 3 * frame_rows
    shape = (frame_rows, LANES)
    lane = lax.broadcasted_iota(jnp.int32, shape, 1)

    def scalar(r, c):
        return jnp.broadcast_to(folded[r : r + 1, c : c + 1], shape)

    def column(j, c):
        return jnp.broadcast_to(folded[j * frame_rows : (j + 1) * frame_rows, c : c + 1], shape)

    total = scalar(tail + 3, base + 3)
    center = [scalar(tail + 3, base + i) / total for i in range(3)]
    frame_center = [column(j, base + 3) / total for j in range(3)]
    x = [
        [column(j, base + i) / total - center[i] * frame_center[j] for j in range(3)]
        for i in range(3)
    ]
    square = sum(x[i][j] * x[i][j] for i in range(3) for j in range(3))
    norm = jnp.sqrt(square)
    x = [[x[i][j] / norm for j in range(3)] for i in range(3)]
    for _ in range(NEWTON):
        cof = [
            [
                x[(i + 1) % 3][(j + 1) % 3] * x[(i + 2) % 3][(j + 2) % 3]
                - x[(i + 1) % 3][(j + 2) % 3] * x[(i + 2) % 3][(j + 1) % 3]
                for j in range(3)
            ]
            for i in range(3)
        ]
        determ = x[0][0] * cof[0][0] + x[0][1] * cof[0][1] + x[0][2] * cof[0][2]
        inverse = 1.0 / determ
        x = [[0.5 * (x[i][j] + cof[i][j] * inverse) for j in range(3)] for i in range(3)]
    shift = [
        center[i] - (x[i][0] * frame_center[0] + x[i][1] * frame_center[1] + x[i][2] * frame_center[2])
        for i in range(3)
    ]
    for i in range(3):
        for j in range(3):
            at = (3 * i + j) * frame_rows
            coef_ref[at : at + frame_rows, :] = x[i][j]
        at = (9 + i) * frame_rows
        coef_ref[at : at + frame_rows, :] = shift[i]

    def by_group(values):
        return jnp.where(lane < vectors, values[0], jnp.where(lane < 2 * vectors, values[1], values[2]))

    y = by_group(shift) * sums[tail + 3 : tail + 4, :]
    y = y - by_group([sums[tail + i : tail + i + 1, :] for i in range(3)])
    for j in range(3):
        block = sums[j * frame_rows : (j + 1) * frame_rows, :]
        y = y + by_group([x[i][j] for i in range(3)]) * block
    y = y + pltpu.roll(y, LANES - vectors, 1) + pltpu.roll(y, LANES - 2 * vectors, 1)
    y = jnp.where(lane < vectors, y, 0.0)
    proj_ref[...] = y


def rotate(parts, frame_rows, vectors):
    return pl.pallas_call(
        functools.partial(rotate_kernel, frame_rows, vectors),
        out_shape=(
            jax.ShapeDtypeStruct((12 * frame_rows, LANES), F32),
            jax.ShapeDtypeStruct((frame_rows, LANES), F32),
        ),
        compiler_params=params(),
        name="rotate",
    )(*parts)


def first_block(chip, line):
    end = jnp.logical_or(chip == 0, chip == line - 1)
    return jnp.where(end, line - 1 - chip, chip)


def displace_kernel(keep, first, line, frame_rows, width, idx, x_ref, m_ref, coef_ref, out_ref):
    core = lax.rem(idx[0], 2)
    side = core if keep else 1 - core
    made_first = first_block(idx[0] // 2, line)

    def coef(i):
        return coef_ref[i * frame_rows : (i + 1) * frame_rows, :]

    def do_block(b, _):
        block = made_first if first else b + (b >= made_first).astype(jnp.int32)
        for start in range(0, width, LANES):
            lanes = pl.ds(pl.multiple_of((2 * block + side) * width + start, LANES), LANES)
            x = [x_ref[j * frame_rows : (j + 1) * frame_rows, lanes] for j in range(3)]
            result = []
            for i in range(3):
                value = coef(3 * i) * x[0] + coef(3 * i + 1) * x[1] + coef(3 * i + 2) * x[2]
                result.append(value + (coef(9 + i) - m_ref[i : i + 1, lanes]))
            to = pl.ds(pl.multiple_of(b * width + start, LANES), LANES)
            out_ref[:, to] = jnp.concatenate(result, axis=0).astype(BF16)
        return 0

    lax.fori_loop(0, 1 if first else line - 1, do_block, 0)


def displace(where_, x, mean, coef, line, keep, first):
    rows, atoms = x.shape
    width = atoms // (2 * line)
    out_width = width if first else (line - 1) * width
    return pl.pallas_call(
        functools.partial(displace_kernel, keep, first, line, rows // 3, width),
        in_specs=[pl.BlockSpec(memory_space=pltpu.SMEM)] + in_vmem(3),
        out_specs=pl.BlockSpec(memory_space=pltpu.VMEM),
        out_shape=jax.ShapeDtypeStruct((rows, out_width), BF16),
        compiler_params=params(),
        name="displace",
    )(where_, x, mean, coef)


def weights_kernel(frame_rows, vectors, own_ref, other_ref, c_ref, e_ref, mean_ref):
    total = jnp.sum(own_ref[...] + other_ref[...], axis=0, keepdims=True)
    mean = total / (2 * frame_rows)
    lane = lax.broadcasted_iota(jnp.int32, (frame_rows, LANES), 1)
    for source, out in ((own_ref, c_ref), (other_ref, e_ref)):
        value = jnp.where(lane < vectors, source[...] - mean, 0.0)
        blocks = [value, pltpu.roll(value, vectors, 1), pltpu.roll(value, 2 * vectors, 1)]
        blocks.append(jnp.zeros((LANES - 3 * frame_rows, LANES), F32))
        table = jnp.concatenate(blocks, axis=0).T
        out[...] = table[0 : 3 * vectors, 0 : 3 * frame_rows].astype(BF16)
    mean_ref[...] = jnp.broadcast_to(jnp.where(lane[0:1] < vectors, mean, 0.0), (8, LANES))


def weights(own, other, frame_rows, vectors):
    out = jax.ShapeDtypeStruct((3 * vectors, 3 * frame_rows), BF16)
    return pl.pallas_call(
        functools.partial(weights_kernel, frame_rows, vectors),
        in_specs=in_vmem(2),
        out_specs=in_vmem(3),
        out_shape=(out, out, jax.ShapeDtypeStruct((8, LANES), F32)),
        compiler_params=params(),
        name="weights",
    )(own, other)


def ones_rows(rows):
    row = lax.broadcasted_iota(jnp.int32, (8, rows), 0)
    column = lax.broadcasted_iota(jnp.int32, (8, rows), 1)
    inside = jnp.logical_and(column >= row * (rows // 3), column < (row + 1) * (rows // 3))
    return jnp.where(inside, 1.0, 0.0).astype(BF16)


def both(left, right, a, b):
    return dot_nn(left, a) + dot_nn(right, b)


def as_column(row, vectors):
    return jnp.broadcast_to(row, (LANES, LANES)).T[0:vectors, 0:1]


def read_slab(slab, width):
    at = 3 * width // LANES
    center = jnp.sum(slab[at : at + 3], axis=0, keepdims=True)
    total = jnp.sum(slab[at + 3 : at + 6], axis=0, keepdims=True)
    return center, total


def write_slab(slab_ref, received, sums, center, total, width):
    tiles = width // LANES
    slab_ref[...] = received
    for i in range(3):
        for tile in range(tiles):
            at = i * tiles + tile
            part = sums[i : i + 1, tile * LANES : (tile + 1) * LANES]
            slab_ref[at : at + 1, :] = received[at : at + 1, :] + part
    for i, piece in enumerate([*split3(center), *split3(total)]):
        at = 3 * tiles + i
        slab_ref[at : at + 1, :] = piece.astype(F32)


def term_kernel(block, starts, line, p, spans, vectors, width, idx, *refs):
    (c_ref, e_ref, mean_ref, a_ref, b_ref), refs = refs[0:5], list(refs[5:])
    slab_ref = refs.pop() if p == 0 else None
    out_ref = refs.pop()
    chip = idx[0] // 2
    if block is None:
        at = 0
    else:
        at = block(chip)
        at = jnp.clip(at - (at > first_block(chip, line)).astype(jnp.int32), 0, line - 2)
    offset, piece_width = spans[p]
    lanes = pl.ds(pl.multiple_of(at * width + offset, LANES), piece_width)
    value = both(c_ref[...], e_ref[...], a_ref[:, lanes], b_ref[:, lanes])
    mean = mean_ref[0:1, :]
    center, total = mean, mean
    slab = jnp.zeros((value.shape[0], LANES), F32)
    ones = ones_rows(a_ref.shape[0])
    if refs:
        slab = refs[0][:, spans[0][1] :].astype(F32)
        center, summed_means = read_slab(slab, width)
        center = jnp.where(starts(chip), mean, center)
        total = mean + summed_means
        column = as_column(mean - center, vectors)
        sums = both(ones, ones, a_ref[:, lanes], b_ref[:, lanes])
        moved = [column * sums[i : i + 1, :] for i in range(3)]
        value = value + jnp.concatenate(moved, axis=0)
        value = value + refs[p][:, 0:piece_width].astype(F32)
    out_ref[:, 0:piece_width] = value.astype(BF16)
    if p == 0:
        lanes = pl.ds(pl.multiple_of(at * width, LANES), width)
        sums = both(ones, ones, a_ref[:, lanes], b_ref[:, lanes])
        write_slab(slab_ref, slab, sums, center, total, width)
        out_ref[:, piece_width:] = slab_ref[...].astype(BF16)


def term(where_, scales, displaced, received, block, starts, line, p, spans, vectors, width):
    rows = scales[0].shape[0]
    args = (*scales, *displaced, *received)
    out_width = spans[p][1] + (LANES if p == 0 else 0)
    return pl.pallas_call(
        functools.partial(term_kernel, block, starts, line, p, spans, vectors, width),
        in_specs=[pl.BlockSpec(memory_space=pltpu.SMEM)] + in_vmem(len(args)),
        out_specs=pl.BlockSpec(memory_space=pltpu.VMEM),
        out_shape=jax.ShapeDtypeStruct((rows, out_width), BF16),
        scratch_shapes=[pltpu.VMEM((rows, LANES), F32)] if p == 0 else [],
        compiler_params=params(),
        cost_estimate=cost(1),
        name="term",
    )(where_, *args)


def inner_products(parts, vectors):
    gram = jnp.zeros((2 * vectors, LANES), F32)
    for part in parts:
        high = part.astype(BF16)
        low = (part - high.astype(F32)).astype(BF16)
        lhs = jnp.concatenate([high, low], axis=0)
        rhs = jnp.concatenate([lhs, jnp.zeros((LANES - 2 * vectors, part.shape[1]), BF16)], axis=0)
        gram = gram + dot_nt(lhs, rhs)
    gram = gram[0:vectors] + gram[vectors : 2 * vectors]
    gram = gram + pltpu.roll(gram, LANES - vectors, 1)
    lane = lax.broadcasted_iota(jnp.int32, gram.shape, 1)
    gram = jnp.where(lane < vectors, gram, 0.0)
    packed = gram[0:8]
    for g in range(1, vectors // 8):
        packed = packed + pltpu.roll(gram[8 * g : 8 * g + 8], vectors * g, 1)
    return packed


def image_kernel(line, spans, vectors, width, frame_count, idx, *refs):
    refs = list(refs)
    c_ref, e_ref, mean_ref = [refs.pop(0) for _ in range(3)]
    firsts, rests = [[refs.pop(0) for _ in range(2)] for _ in range(2)]
    old_ref = refs.pop(0)
    image_ref, gram_ref, new_mean_ref, next_ref, block_ref = refs[-5:]
    received = refs[:-5]
    chip = idx[0] // 2
    made_first = first_block(chip, line)
    at = jnp.clip(chip - (chip > made_first).astype(jnp.int32), 0, line - 2) * width
    for n in range(2):

        @pl.when(chip == made_first)
        def _(n=n):
            block_ref[n] = firsts[n][...]

        @pl.when(chip != made_first)
        def _(n=n):
            block_ref[n] = rests[n][:, pl.ds(pl.multiple_of(at, LANES), width)]

    ones = ones_rows(block_ref.shape[1])
    sums = both(ones, ones, block_ref[0], block_ref[1])
    mean = mean_ref[0:1, :]
    slabs = [ref[:, spans[0][1] :].astype(F32) for ref in received]
    centers, totals = zip(*(read_slab(slab, width) for slab in slabs))
    center = functools.reduce(jnp.add, totals, mean) / line
    columns = [as_column(v - center, vectors) for v in (mean, *centers)]
    tiles = width // LANES

    def own_part(offset, piece_width):
        lanes = slice(offset, offset + piece_width)
        value = both(c_ref[...], e_ref[...], block_ref[0, :, lanes], block_ref[1, :, lanes])
        parts = []
        for i in range(3):
            moved = []
            for tile in range(offset // LANES, (offset + piece_width) // LANES):
                part = columns[0] * sums[i : i + 1, tile * LANES : (tile + 1) * LANES]
                row = i * tiles + tile
                for column, slab in zip(columns[1:], slabs):
                    part = part + column * slab[row : row + 1, :]
                moved.append(part)
            rows = slice(i * vectors, (i + 1) * vectors)
            parts.append(value[rows] + jnp.concatenate(moved, axis=1))
        return parts

    piece_width = spans[0][1]
    parts = own_part(*spans[0])
    for i in range(3):
        rows = slice(i * vectors, (i + 1) * vectors)
        for ref in received:
            parts[i] = parts[i] + ref[rows, 0:piece_width].astype(F32)
        parts[i] = parts[i] / frame_count
        image_ref[rows, :] = parts[i]
    gram_ref[...] = inner_products(parts, vectors)
    for i, part in enumerate(own_part(*spans[1])):
        next_ref[i * vectors : (i + 1) * vectors, :] = part
    total = functools.reduce(jnp.add, slabs)
    for i in range(3):
        for tile in range(tiles):
            start = (idx[0] * tiles + tile) * LANES
            old = old_ref[i : i + 1, pl.ds(pl.multiple_of(start, LANES), LANES)]
            row = i * tiles + tile
            here = slice(tile * LANES, (tile + 1) * LANES)
            added = (total[row : row + 1, :] + sums[i : i + 1, here]) / frame_count
            new_mean_ref[i : i + 1, here] = old + added


def first_piece(where_, scales, firsts, rests, mean, received, line, spans, vectors, width, frame_count):
    rows = scales[0].shape[0]
    args = (*scales, *firsts, *rests, mean, *received)
    shapes = ((rows, spans[0][1]), (8, LANES), (3, width), (rows, spans[1][1]))
    return pl.pallas_call(
        functools.partial(image_kernel, line, spans, vectors, width, frame_count),
        in_specs=[pl.BlockSpec(memory_space=pltpu.SMEM)] + in_vmem(len(args)),
        out_specs=in_vmem(len(shapes)),
        out_shape=[jax.ShapeDtypeStruct(shape, F32) for shape in shapes],
        scratch_shapes=[pltpu.VMEM((2, firsts[0].shape[0], width), BF16)],
        compiler_params=params(),
        cost_estimate=cost(2),
        name="first_piece",
    )(where_, *args)


def finish_kernel(vectors, frame_count, own_ref, before_ref, *refs):
    received, (image_ref, gram_ref) = refs[:-2], refs[-2:]
    parts = []
    for i in range(3):
        rows = slice(i * vectors, (i + 1) * vectors)
        part = own_ref[rows, :]
        for ref in received:
            part = part + ref[rows, :].astype(F32)
        parts.append(part / frame_count)
        image_ref[rows, :] = parts[i]
    gram_ref[...] = before_ref[...] + inner_products(parts, vectors)


def second_piece(own, gram, received, vectors, frame_count):
    args = (own, gram, *received)
    return pl.pallas_call(
        functools.partial(finish_kernel, vectors, frame_count),
        in_specs=in_vmem(len(args)),
        out_specs=in_vmem(2),
        out_shape=[jax.ShapeDtypeStruct(v.shape, F32) for v in (own, gram)],
        compiler_params=params(),
        name="second_piece",
    )(*args)


def fold_kernel(*refs):
    value = refs[0][...]
    for ref in refs[1:-1]:
        value = value + ref[...]
    refs[-1][...] = value


def fold(parts):
    return pl.pallas_call(
        fold_kernel,
        in_specs=in_vmem(len(parts)),
        out_specs=pl.BlockSpec(memory_space=pltpu.VMEM),
        out_shape=jax.ShapeDtypeStruct(parts[0].shape, F32),
        compiler_params=params(),
        name="fold",
    )(*parts)


def exchanged(value, axis, size, bits):
    masks = [0]
    for bit in bits:
        masks += [mask | (1 << bit) for mask in masks]
    return [value] + [
        lax.ppermute(value, axis, [(i, i ^ mask) for i in range(size)]) for mask in masks[:0:-1]
    ]


def summed(value, axis, size, bits):
    groups = [bits[start : start + 2] for start in range(0, len(bits), 2)]
    for group in groups[:-1]:
        value = fold(exchanged(value, axis, size, group))
    return exchanged(value, axis, size, groups[-1])


def basis_kernel(vectors, coordinates, gram_count, *refs):
    grams, pieces = refs[:gram_count], refs[gram_count:-4]
    image_hbm, basis_hbm, basis_ref, sems = refs[-4:]
    copies, starts = [], [0]
    for n, ref in enumerate(pieces):
        starts.append(starts[n] + ref.shape[1])
        lanes = pl.ds(starts[n], ref.shape[1])
        copies.append(pltpu.make_async_copy(ref, image_hbm.at[:, lanes], sems.at[n, 3]))
        copies[-1].start()
    packed = grams[0][...]
    for ref in grams[1:]:
        packed = packed + ref[...]
    packed = packed / coordinates
    groups = [packed]
    for g in range(1, vectors // 8):
        groups.append(pltpu.roll(packed, LANES - vectors * g, 1))
    gram = jnp.concatenate(groups, axis=0)
    row = lax.broadcasted_iota(jnp.int32, gram.shape, 0)
    lane = lax.broadcasted_iota(jnp.int32, gram.shape, 1)
    a = jnp.where(lane < vectors, gram, jnp.where(lane == row + vectors, 1.0, 0.0))
    for panel in range(0, vectors, PANEL):
        columns = [
            jnp.broadcast_to(a[:, j : j + 1], a.shape) for j in range(panel, panel + PANEL)
        ]
        for q in range(PANEL):
            j = panel + q
            factor = columns[q] * (1.0 / columns[q][j : j + 1, :])
            factor = jnp.where(row > j, factor, 0.0)
            for r in range(q + 1, PANEL):
                columns[r] = columns[r] - factor * columns[r][j : j + 1, :]
            a = a - factor * a[j : j + 1, :]
    diagonal = jnp.sum(jnp.where(lane == row, a, 0.0), axis=1, keepdims=True)
    a = a * (1.0 / jnp.sqrt(diagonal))
    a = jnp.where(lane < vectors, pltpu.roll(a, LANES - vectors, 1), 0.0)
    high = a.astype(BF16).astype(F32)
    left = high + pltpu.roll(high, vectors, 1) + pltpu.roll(a - high, 2 * vectors, 1)
    left = left.astype(BF16)[:, 0 : 3 * vectors]
    for n, ref in enumerate(pieces):
        for i in range(3):
            rows, lanes = pl.ds(i * vectors, vectors), pl.ds(starts[n], ref.shape[1])
            part = ref[rows, :]
            high = part.astype(BF16)
            low = (part - high.astype(F32)).astype(BF16)
            basis_ref[rows, lanes] = dot_nn(left, jnp.concatenate([high, low, high], axis=0))
            copies.append(
                pltpu.make_async_copy(
                    basis_ref.at[rows, lanes], basis_hbm.at[rows, lanes], sems.at[n, i]
                )
            )
            copies[-1].start()
    for copy in copies:
        copy.wait()


def basis_of(grams, images, vectors, coordinates):
    rows = images[0].shape[0]
    width = sum(v.shape[1] for v in images)
    return pl.pallas_call(
        functools.partial(basis_kernel, vectors, coordinates, len(grams)),
        in_specs=in_vmem(len(grams) + len(images)),
        out_specs=[pl.BlockSpec(memory_space=pl.ANY)] * 2,
        out_shape=[jax.ShapeDtypeStruct((rows, width), F32)] * 2,
        scratch_shapes=[
            pltpu.VMEM((rows, width), F32),
            pltpu.SemaphoreType.DMA((len(images), 4)),
        ],
        compiler_params=params(),
        name="basis",
    )(*grams, *images)


def to_right(z):
    return [(2 * z + core, 2 * z + 2 + core) for core in range(2)]


def to_left(z):
    return [(2 * z + core, 2 * z - 2 + core) for core in range(2)]


def along_four(pieces, make_first, make):
    inward, middle, outward = (to_right(z) + to_left(3 - z) for z in range(3))

    def at_end(chip):
        return jnp.logical_or(chip == 0, chip == 3)

    def never(chip):
        return chip < 0

    def choose(*blocks):
        def block(chip):
            return sum(jnp.where(chip == z, d, 0) for z, d in enumerate(blocks))

        return block

    each = range(pieces)
    first = [lax.ppermute(make_first(p), "frames", inward) for p in each]
    ends, middles = [], []
    for p in each:
        out = make((), choose(2, 0, 0, 1), None, p, first[p])
        ends.append(lax.ppermute(out, "frames", inward))
        out = make(first[: p + 1], choose(0, 3, 0, 0), never, p)
        middles.append(lax.ppermute(out, "frames", middle))
    arrived = []
    for p in each:
        out = make(middles[: p + 1], choose(1, 0, 3, 2), at_end, p, ends[p])
        end = lax.ppermute(out, "frames", inward + outward)
        out = make(ends[: p + 1], choose(0, 2, 1, 0), never, p, out)
        arrived.append([end, lax.ppermute(out, "frames", middle)])
    return arrived


def along_line(line, pieces, make_first, make):
    ends = to_right(0) + to_left(line - 1)
    right = [lax.ppermute(make_first(p), "frames", ends) for p in range(pieces)]
    left = list(right)
    for step in range(2, line):

        def right_block(chip, step=step):
            return jnp.minimum(line - step + chip, line - 1)

        def left_block(chip, step=step):
            return jnp.maximum(step - line + chip, 0)

        right_pairs = [pair for z in range(step) for pair in to_right(z)]
        left_pairs = [pair for z in range(step) for pair in to_left(line - 1 - z)]
        next_right, next_left = [], []
        for p in range(pieces):
            out = make(right[: p + 1], right_block, lambda chip: chip == 0, p)
            next_right.append(lax.ppermute(out, "frames", right_pairs))
            out = make(left[: p + 1], left_block, lambda chip: chip == line - 1, p)
            next_left.append(lax.ppermute(out, "frames", left_pairs))
        right, left = next_right, next_left
    return [[right[p], left[p]] for p in range(pieces)]


def per_device(atom_devices, frame_devices, frames, mean_structure, atom_weight, subspace):
    frame_rows, _, atoms = frames.shape
    vectors = subspace.shape[0]
    frame_count = frame_rows * frame_devices
    width = atoms // frame_devices
    line = frame_devices // 2
    tiles = width // LANES
    assert line > 2 and tiles > 1 and 3 * tiles + 6 <= 3 * vectors
    cut = tiles // 2 * LANES
    spans = ((0, cut), (cut, width - cut))

    x = jnp.transpose(frames, (1, 0, 2)).reshape(3 * frame_rows, atoms)
    sub = jnp.transpose(subspace, (1, 0, 2)).reshape(3 * vectors, atoms)
    where_ = lax.axis_index("frames").astype(jnp.int32).reshape(1)

    inputs = (x, mean_structure, atom_weight.reshape(1, atoms), sub)
    local, x = moments(where_, *(pltpu.with_memory_space_constraint(v, pltpu.HBM) for v in inputs))
    atom_bits = range(atom_devices.bit_length() - 1)
    coef, proj = rotate(summed(local, "atoms", atom_devices, atom_bits), frame_rows, vectors)

    swap = [(i, i ^ 1) for i in range(frame_devices)]
    proj_other = lax.ppermute(proj, "frames", swap)

    def made(keep, first, after):
        late = lax.optimization_barrier((coef, after))[0]
        return displace(where_, x, mean_structure, late, line, keep, first)

    first_sent = made(False, True, proj)
    first_own = made(True, True, first_sent)
    firsts = (first_own, lax.ppermute(first_sent, "frames", swap))
    rest_sent = made(False, False, first_own)
    rest_sent = lax.optimization_barrier((rest_sent, firsts[1], proj_other))[0]
    rest_other = lax.ppermute(rest_sent, "frames", swap)
    scales = weights(proj, proj_other, frame_rows, vectors)

    last, kept = None, []

    def make_first(p):
        nonlocal last
        last = term(where_, scales, firsts, (), None, None, line, p, spans, vectors, width)
        return last

    def rests():
        if not kept:
            kept.append(made(True, False, last))
        return kept[0], rest_other

    def make(received, block, starts, p, after=None):
        late = scales
        if after is not None:
            late = lax.optimization_barrier((scales, after))[0]
        return term(where_, late, rests(), received, block, starts, line, p, spans, vectors, width)

    if line == 4:
        arrived = along_four(len(spans), make_first, make)
    else:
        arrived = along_line(line, len(spans), make_first, make)
    image, gram, new_mean, second = first_piece(
        where_, scales, firsts, rests(), mean_structure, arrived[0], line, spans, vectors, width,
        frame_count,
    )
    images = [image]
    image, gram = second_piece(second, gram, arrived[1], vectors, frame_count)
    images.append(image)
    gram = fold(summed(gram, "atoms", atom_devices, atom_bits))
    gram = fold(exchanged(gram, "frames", frame_devices, [0]))
    grams = summed(gram, "frames", frame_devices, range(1, frame_devices.bit_length() - 1))
    image, basis = basis_of(grams, images, vectors, 3 * atoms * atom_devices)

    def placed(value):
        return jnp.transpose(value.reshape(3, vectors, width), (1, 0, 2))

    return new_mean, placed(image), placed(basis)


def solution(mesh):
    return jax.shard_map(
        functools.partial(per_device, mesh.shape["atoms"], mesh.shape["frames"]),
        mesh=mesh,
        in_specs=(P("frames", None, "atoms"), P(None, "atoms"), P("atoms"), P(None, None, "atoms")),
        out_specs=(
            P(None, ("atoms", "frames")),
            P(None, None, ("atoms", "frames")),
            P(None, None, ("atoms", "frames")),
        ),
        check_vma=False,
    )
```

```python
import functools

import jax
import jax.numpy as jnp
from jax import lax
from jax.experimental import pallas as pl
from jax.experimental.pallas import tpu as pltpu
from jax.sharding import PartitionSpec as P

NEWTON = 8
LANES = 128
F32 = jnp.float32
BF16 = jnp.bfloat16
TILE = 256
PANEL = 4
VMEM_LIMIT = 24 * 1024 * 1024


def params():
    return pltpu.CompilerParams(vmem_limit_bytes=VMEM_LIMIT)


def cost(weight):
    return pl.CostEstimate(flops=weight * 10**9, bytes_accessed=1, transcendentals=0)


def in_vmem(count):
    return [pl.BlockSpec(memory_space=pltpu.VMEM)] * count


def split3(value):
    high = value.astype(BF16)
    rest = value - high.astype(F32)
    middle = rest.astype(BF16)
    low = (rest - middle.astype(F32)).astype(BF16)
    return high, middle, low


def dot_nt(a, b):
    return lax.dot_general(a, b, (((1,), (1,)), ((), ())), preferred_element_type=F32)


def dot_nn(a, b, precision=None):
    return lax.dot_general(
        a, b, (((1,), (0,)), ((), ())), preferred_element_type=F32, precision=precision
    )


def moments_kernel(
    _, x_hbm, m_hbm, w_hbm, s_hbm, out_ref, x_ref, m_ref, w_ref, lhs_ref, rhs_ref, sems
):
    rows, atoms = x_ref.shape
    vectors = s_hbm.shape[0]
    chunks = sems.shape[1] - 1
    chunk = atoms // chunks
    n = rows + 8
    copies = [
        [
            pltpu.make_async_copy(m_hbm, m_ref, sems.at[0, chunks]),
            pltpu.make_async_copy(w_hbm, w_ref, sems.at[1, chunks]),
        ]
    ]
    for t in range(chunks):
        lanes = pl.ds(t * chunk, chunk)
        copies.append(
            [
                pltpu.make_async_copy(x_hbm.at[:, lanes], x_ref.at[:, lanes], sems.at[0, t]),
                pltpu.make_async_copy(
                    s_hbm.at[:, lanes], rhs_ref.at[0:vectors, lanes], sems.at[1, t]
                ),
            ]
        )
    for group in copies:
        for copy in group:
            copy.start()
    for copy in copies[0]:
        copy.wait()
    row = lax.broadcasted_iota(jnp.int32, (8, TILE), 0)
    ones = jnp.where(row == 3, 1.0, 0.0)
    total = jnp.zeros(out_ref.shape, F32)
    for t in range(chunks):
        for copy in copies[t + 1]:
            copy.wait()
        slot, half = t // 2 % 2, t % 2 * chunk
        for start in range(0, chunk, TILE):
            lanes = slice(t * chunk + start, t * chunk + start + TILE)
            here = slice(half + start, half + start + TILE)
            left = ones
            for i in range(3):
                left = jnp.where(row == i, m_ref[i : i + 1, lanes], left)
            value = jnp.concatenate([x_ref[:, lanes], left], axis=0)
            high = value.astype(BF16)
            lhs_ref[slot, 0:n, here] = high
            lhs_ref[slot, n : 2 * n, here] = (value - high.astype(F32)).astype(BF16)
            pieces = [v.astype(F32) for v in split3(left * w_ref[:, lanes])]
            aux = jnp.concatenate(pieces + [jnp.zeros(left.shape, F32)], axis=0)
            rhs_ref[vectors:, lanes] = aux.astype(BF16)
        if t % 2 == 1:
            sums = dot_nt(lhs_ref[slot], rhs_ref[:, (t - 1) * chunk : (t + 1) * chunk])
            total = total + (sums[0:n] + sums[n : 2 * n])
    out_ref[...] = total


def moments(where_, x, mean, weight, sub):
    rows, atoms = x.shape
    vectors = sub.shape[0]
    chunks = 16
    chunk = atoms // chunks
    n = rows + 8
    return pl.pallas_call(
        moments_kernel,
        in_specs=[pl.BlockSpec(memory_space=pltpu.SMEM)] + [pl.BlockSpec(memory_space=pl.ANY)] * 4,
        out_specs=in_vmem(2),
        out_shape=(jax.ShapeDtypeStruct((n, LANES), F32), jax.ShapeDtypeStruct(x.shape, F32)),
        scratch_shapes=[
            pltpu.VMEM(mean.shape, F32),
            pltpu.VMEM(weight.shape, F32),
            pltpu.VMEM((2, 2 * n, 2 * chunk), BF16),
            pltpu.VMEM((LANES, atoms), BF16),
            pltpu.SemaphoreType.DMA((2, chunks + 1)),
        ],
        compiler_params=params(),
        name="moments",
    )(where_, x, mean, weight, sub)


def rotate_kernel(frame_rows, vectors, *refs):
    parts, (coef_ref, proj_ref) = refs[:-2], refs[-2:]
    sums = parts[0][...]
    for ref in parts[1:]:
        sums = sums + ref[...]
    folded = sums + pltpu.roll(sums, LANES - 8, 1) + pltpu.roll(sums, LANES - 16, 1)
    base = 3 * vectors
    tail = 3 * frame_rows
    shape = (frame_rows, LANES)
    lane = lax.broadcasted_iota(jnp.int32, shape, 1)

    def scalar(r, c):
        return jnp.broadcast_to(folded[r : r + 1, c : c + 1], shape)

    def column(j, c):
        return jnp.broadcast_to(folded[j * frame_rows : (j + 1) * frame_rows, c : c + 1], shape)

    total = scalar(tail + 3, base + 3)
    center = [scalar(tail + 3, base + i) / total for i in range(3)]
    frame_center = [column(j, base + 3) / total for j in range(3)]
    x = [
        [column(j, base + i) / total - center[i] * frame_center[j] for j in range(3)]
        for i in range(3)
    ]
    square = sum(x[i][j] * x[i][j] for i in range(3) for j in range(3))
    norm = jnp.sqrt(square)
    x = [[x[i][j] / norm for j in range(3)] for i in range(3)]
    for _ in range(NEWTON):
        cof = [
            [
                x[(i + 1) % 3][(j + 1) % 3] * x[(i + 2) % 3][(j + 2) % 3]
                - x[(i + 1) % 3][(j + 2) % 3] * x[(i + 2) % 3][(j + 1) % 3]
                for j in range(3)
            ]
            for i in range(3)
        ]
        determ = x[0][0] * cof[0][0] + x[0][1] * cof[0][1] + x[0][2] * cof[0][2]
        inverse = 1.0 / determ
        x = [[0.5 * (x[i][j] + cof[i][j] * inverse) for j in range(3)] for i in range(3)]
    shift = [
        center[i] - (x[i][0] * frame_center[0] + x[i][1] * frame_center[1] + x[i][2] * frame_center[2])
        for i in range(3)
    ]
    for i in range(3):
        for j in range(3):
            at = (3 * i + j) * frame_rows
            coef_ref[at : at + frame_rows, :] = x[i][j]
        at = (9 + i) * frame_rows
        coef_ref[at : at + frame_rows, :] = shift[i]

    def by_group(values):
        return jnp.where(lane < vectors, values[0], jnp.where(lane < 2 * vectors, values[1], values[2]))

    y = by_group(shift) * sums[tail + 3 : tail + 4, :]
    y = y - by_group([sums[tail + i : tail + i + 1, :] for i in range(3)])
    for j in range(3):
        block = sums[j * frame_rows : (j + 1) * frame_rows, :]
        y = y + by_group([x[i][j] for i in range(3)]) * block
    y = y + pltpu.roll(y, LANES - vectors, 1) + pltpu.roll(y, LANES - 2 * vectors, 1)
    y = jnp.where(lane < vectors, y, 0.0)
    proj_ref[...] = y


def rotate(parts, frame_rows, vectors):
    return pl.pallas_call(
        functools.partial(rotate_kernel, frame_rows, vectors),
        out_shape=(
            jax.ShapeDtypeStruct((12 * frame_rows, LANES), F32),
            jax.ShapeDtypeStruct((frame_rows, LANES), F32),
        ),
        compiler_params=params(),
        name="rotate",
    )(*parts)


def first_block(chip, line):
    end = jnp.logical_or(chip == 0, chip == line - 1)
    return jnp.where(end, line - 1 - chip, chip)


def displace_kernel(keep, first, line, frame_rows, width, idx, x_ref, m_ref, coef_ref, out_ref):
    core = lax.rem(idx[0], 2)
    side = core if keep else 1 - core
    made_first = first_block(idx[0] // 2, line)

    def coef(i):
        return coef_ref[i * frame_rows : (i + 1) * frame_rows, :]

    def do_block(b, _):
        block = made_first if first else b + (b >= made_first).astype(jnp.int32)
        for start in range(0, width, LANES):
            lanes = pl.ds(pl.multiple_of((2 * block + side) * width + start, LANES), LANES)
            x = [x_ref[j * frame_rows : (j + 1) * frame_rows, lanes] for j in range(3)]
            result = []
            for i in range(3):
                value = coef(3 * i) * x[0] + coef(3 * i + 1) * x[1] + coef(3 * i + 2) * x[2]
                result.append(value + (coef(9 + i) - m_ref[i : i + 1, lanes]))
            to = pl.ds(pl.multiple_of(b * width + start, LANES), LANES)
            out_ref[:, to] = jnp.concatenate(result, axis=0).astype(BF16)
        return 0

    lax.fori_loop(0, 1 if first else line - 1, do_block, 0)


def displace(where_, x, mean, coef, line, keep, first):
    rows, atoms = x.shape
    width = atoms // (2 * line)
    out_width = width if first else (line - 1) * width
    return pl.pallas_call(
        functools.partial(displace_kernel, keep, first, line, rows // 3, width),
        in_specs=[pl.BlockSpec(memory_space=pltpu.SMEM)] + in_vmem(3),
        out_specs=pl.BlockSpec(memory_space=pltpu.VMEM),
        out_shape=jax.ShapeDtypeStruct((rows, out_width), BF16),
        compiler_params=params(),
        name="displace",
    )(where_, x, mean, coef)


def weights_kernel(frame_rows, vectors, own_ref, other_ref, c_ref, e_ref, mean_ref):
    total = jnp.sum(own_ref[...] + other_ref[...], axis=0, keepdims=True)
    mean = total / (2 * frame_rows)
    lane = lax.broadcasted_iota(jnp.int32, (frame_rows, LANES), 1)
    for source, out in ((own_ref, c_ref), (other_ref, e_ref)):
        value = jnp.where(lane < vectors, source[...] - mean, 0.0)
        blocks = [value, pltpu.roll(value, vectors, 1), pltpu.roll(value, 2 * vectors, 1)]
        blocks.append(jnp.zeros((LANES - 3 * frame_rows, LANES), F32))
        table = jnp.concatenate(blocks, axis=0).T
        out[...] = table[0 : 3 * vectors, 0 : 3 * frame_rows].astype(BF16)
    mean_ref[...] = jnp.broadcast_to(jnp.where(lane[0:1] < vectors, mean, 0.0), (8, LANES))


def weights(own, other, frame_rows, vectors):
    out = jax.ShapeDtypeStruct((3 * vectors, 3 * frame_rows), BF16)
    return pl.pallas_call(
        functools.partial(weights_kernel, frame_rows, vectors),
        in_specs=in_vmem(2),
        out_specs=in_vmem(3),
        out_shape=(out, out, jax.ShapeDtypeStruct((8, LANES), F32)),
        compiler_params=params(),
        name="weights",
    )(own, other)


def ones_rows(rows):
    row = lax.broadcasted_iota(jnp.int32, (8, rows), 0)
    column = lax.broadcasted_iota(jnp.int32, (8, rows), 1)
    inside = jnp.logical_and(column >= row * (rows // 3), column < (row + 1) * (rows // 3))
    return jnp.where(inside, 1.0, 0.0).astype(BF16)


def both(left, right, a, b):
    return dot_nn(left, a) + dot_nn(right, b)


def as_column(row, vectors):
    return jnp.broadcast_to(row, (LANES, LANES)).T[0:vectors, 0:1]


def read_slab(slab, width):
    at = 3 * width // LANES
    center = jnp.sum(slab[at : at + 3], axis=0, keepdims=True)
    total = jnp.sum(slab[at + 3 : at + 6], axis=0, keepdims=True)
    return center, total


def write_slab(slab_ref, received, sums, center, total, width):
    tiles = width // LANES
    slab_ref[...] = received
    for i in range(3):
        for tile in range(tiles):
            at = i * tiles + tile
            part = sums[i : i + 1, tile * LANES : (tile + 1) * LANES]
            slab_ref[at : at + 1, :] = received[at : at + 1, :] + part
    for i, piece in enumerate([*split3(center), *split3(total)]):
        at = 3 * tiles + i
        slab_ref[at : at + 1, :] = piece.astype(F32)


def term_kernel(block, starts, line, p, spans, vectors, width, idx, *refs):
    (c_ref, e_ref, mean_ref, a_ref, b_ref), refs = refs[0:5], list(refs[5:])
    slab_ref = refs.pop() if p == 0 else None
    out_ref = refs.pop()
    chip = idx[0] // 2
    if block is None:
        at = 0
    else:
        at = block(chip)
        at = jnp.clip(at - (at > first_block(chip, line)).astype(jnp.int32), 0, line - 2)
    offset, piece_width = spans[p]
    lanes = pl.ds(pl.multiple_of(at * width + offset, LANES), piece_width)
    value = both(c_ref[...], e_ref[...], a_ref[:, lanes], b_ref[:, lanes])
    mean = mean_ref[0:1, :]
    center, total = mean, mean
    slab = jnp.zeros((value.shape[0], LANES), F32)
    ones = ones_rows(a_ref.shape[0])
    if refs:
        slab = refs[0][:, spans[0][1] :].astype(F32)
        center, summed_means = read_slab(slab, width)
        center = jnp.where(starts(chip), mean, center)
        total = mean + summed_means
        column = as_column(mean - center, vectors)
        sums = both(ones, ones, a_ref[:, lanes], b_ref[:, lanes])
        moved = [column * sums[i : i + 1, :] for i in range(3)]
        value = value + jnp.concatenate(moved, axis=0)
        value = value + refs[p][:, 0:piece_width].astype(F32)
    out_ref[:, 0:piece_width] = value.astype(BF16)
    if p == 0:
        lanes = pl.ds(pl.multiple_of(at * width, LANES), width)
        sums = both(ones, ones, a_ref[:, lanes], b_ref[:, lanes])
        write_slab(slab_ref, slab, sums, center, total, width)
        out_ref[:, piece_width:] = slab_ref[...].astype(BF16)


def term(where_, scales, displaced, received, block, starts, line, p, spans, vectors, width):
    rows = scales[0].shape[0]
    args = (*scales, *displaced, *received)
    out_width = spans[p][1] + (LANES if p == 0 else 0)
    return pl.pallas_call(
        functools.partial(term_kernel, block, starts, line, p, spans, vectors, width),
        in_specs=[pl.BlockSpec(memory_space=pltpu.SMEM)] + in_vmem(len(args)),
        out_specs=pl.BlockSpec(memory_space=pltpu.VMEM),
        out_shape=jax.ShapeDtypeStruct((rows, out_width), BF16),
        scratch_shapes=[pltpu.VMEM((rows, LANES), F32)] if p == 0 else [],
        compiler_params=params(),
        cost_estimate=cost(1),
        name="term",
    )(where_, *args)


def inner_products(parts, vectors):
    gram = jnp.zeros((2 * vectors, LANES), F32)
    for part in parts:
        high = part.astype(BF16)
        low = (part - high.astype(F32)).astype(BF16)
        lhs = jnp.concatenate([high, low], axis=0)
        rhs = jnp.concatenate([lhs, jnp.zeros((LANES - 2 * vectors, part.shape[1]), BF16)], axis=0)
        gram = gram + dot_nt(lhs, rhs)
    gram = gram[0:vectors] + gram[vectors : 2 * vectors]
    gram = gram + pltpu.roll(gram, LANES - vectors, 1)
    lane = lax.broadcasted_iota(jnp.int32, gram.shape, 1)
    gram = jnp.where(lane < vectors, gram, 0.0)
    packed = gram[0:8]
    for g in range(1, vectors // 8):
        packed = packed + pltpu.roll(gram[8 * g : 8 * g + 8], vectors * g, 1)
    return packed


def image_kernel(line, spans, vectors, width, frame_count, idx, *refs):
    refs = list(refs)
    c_ref, e_ref, mean_ref = [refs.pop(0) for _ in range(3)]
    firsts, rests = [[refs.pop(0) for _ in range(2)] for _ in range(2)]
    old_ref = refs.pop(0)
    image_ref, gram_ref, new_mean_ref, next_ref, block_ref = refs[-5:]
    received = refs[:-5]
    chip = idx[0] // 2
    made_first = first_block(chip, line)
    at = jnp.clip(chip - (chip > made_first).astype(jnp.int32), 0, line - 2) * width
    for n in range(2):

        @pl.when(chip == made_first)
        def _(n=n):
            block_ref[n] = firsts[n][...]

        @pl.when(chip != made_first)
        def _(n=n):
            block_ref[n] = rests[n][:, pl.ds(pl.multiple_of(at, LANES), width)]

    ones = ones_rows(block_ref.shape[1])
    sums = both(ones, ones, block_ref[0], block_ref[1])
    mean = mean_ref[0:1, :]
    slabs = [ref[:, spans[0][1] :].astype(F32) for ref in received]
    centers, totals = zip(*(read_slab(slab, width) for slab in slabs))
    center = functools.reduce(jnp.add, totals, mean) / line
    columns = [as_column(v - center, vectors) for v in (mean, *centers)]
    tiles = width // LANES

    def own_part(offset, piece_width):
        lanes = slice(offset, offset + piece_width)
        value = both(c_ref[...], e_ref[...], block_ref[0, :, lanes], block_ref[1, :, lanes])
        parts = []
        for i in range(3):
            moved = []
            for tile in range(offset // LANES, (offset + piece_width) // LANES):
                part = columns[0] * sums[i : i + 1, tile * LANES : (tile + 1) * LANES]
                row = i * tiles + tile
                for column, slab in zip(columns[1:], slabs):
                    part = part + column * slab[row : row + 1, :]
                moved.append(part)
            rows = slice(i * vectors, (i + 1) * vectors)
            parts.append(value[rows] + jnp.concatenate(moved, axis=1))
        return parts

    piece_width = spans[0][1]
    parts = own_part(*spans[0])
    for i in range(3):
        rows = slice(i * vectors, (i + 1) * vectors)
        for ref in received:
            parts[i] = parts[i] + ref[rows, 0:piece_width].astype(F32)
        parts[i] = parts[i] / frame_count
        image_ref[rows, :] = parts[i]
    gram_ref[...] = inner_products(parts, vectors)
    for i, part in enumerate(own_part(*spans[1])):
        next_ref[i * vectors : (i + 1) * vectors, :] = part
    total = functools.reduce(jnp.add, slabs)
    for i in range(3):
        for tile in range(tiles):
            start = (idx[0] * tiles + tile) * LANES
            old = old_ref[i : i + 1, pl.ds(pl.multiple_of(start, LANES), LANES)]
            row = i * tiles + tile
            here = slice(tile * LANES, (tile + 1) * LANES)
            added = (total[row : row + 1, :] + sums[i : i + 1, here]) / frame_count
            new_mean_ref[i : i + 1, here] = old + added


def first_piece(where_, scales, firsts, rests, mean, received, line, spans, vectors, width, frame_count):
    rows = scales[0].shape[0]
    args = (*scales, *firsts, *rests, mean, *received)
    shapes = ((rows, spans[0][1]), (8, LANES), (3, width), (rows, spans[1][1]))
    return pl.pallas_call(
        functools.partial(image_kernel, line, spans, vectors, width, frame_count),
        in_specs=[pl.BlockSpec(memory_space=pltpu.SMEM)] + in_vmem(len(args)),
        out_specs=in_vmem(len(shapes)),
        out_shape=[jax.ShapeDtypeStruct(shape, F32) for shape in shapes],
        scratch_shapes=[pltpu.VMEM((2, firsts[0].shape[0], width), BF16)],
        compiler_params=params(),
        cost_estimate=cost(2),
        name="first_piece",
    )(where_, *args)


def finish_kernel(vectors, frame_count, own_ref, before_ref, *refs):
    received, (image_ref, gram_ref) = refs[:-2], refs[-2:]
    parts = []
    for i in range(3):
        rows = slice(i * vectors, (i + 1) * vectors)
        part = own_ref[rows, :]
        for ref in received:
            part = part + ref[rows, :].astype(F32)
        parts.append(part / frame_count)
        image_ref[rows, :] = parts[i]
    gram_ref[...] = before_ref[...] + inner_products(parts, vectors)


def second_piece(own, gram, received, vectors, frame_count):
    args = (own, gram, *received)
    return pl.pallas_call(
        functools.partial(finish_kernel, vectors, frame_count),
        in_specs=in_vmem(len(args)),
        out_specs=in_vmem(2),
        out_shape=[jax.ShapeDtypeStruct(v.shape, F32) for v in (own, gram)],
        compiler_params=params(),
        name="second_piece",
    )(*args)


def fold_kernel(*refs):
    value = refs[0][...]
    for ref in refs[1:-1]:
        value = value + ref[...]
    refs[-1][...] = value


def fold(parts):
    return pl.pallas_call(
        fold_kernel,
        in_specs=in_vmem(len(parts)),
        out_specs=pl.BlockSpec(memory_space=pltpu.VMEM),
        out_shape=jax.ShapeDtypeStruct(parts[0].shape, F32),
        compiler_params=params(),
        name="fold",
    )(*parts)


def exchanged(value, axis, size, bits):
    masks = [0]
    for bit in bits:
        masks += [mask | (1 << bit) for mask in masks]
    return [value] + [
        lax.ppermute(value, axis, [(i, i ^ mask) for i in range(size)]) for mask in masks[:0:-1]
    ]


def summed(value, axis, size, bits):
    groups = [bits[start : start + 2] for start in range(0, len(bits), 2)]
    for group in groups[:-1]:
        value = fold(exchanged(value, axis, size, group))
    return exchanged(value, axis, size, groups[-1])


def basis_kernel(vectors, coordinates, gram_count, *refs):
    grams, pieces = refs[:gram_count], refs[gram_count:-4]
    image_hbm, basis_hbm, basis_ref, sems = refs[-4:]
    copies, starts = [], [0]
    for n, ref in enumerate(pieces):
        starts.append(starts[n] + ref.shape[1])
        lanes = pl.ds(starts[n], ref.shape[1])
        copies.append(pltpu.make_async_copy(ref, image_hbm.at[:, lanes], sems.at[n, 3]))
        copies[-1].start()
    packed = grams[0][...]
    for ref in grams[1:]:
        packed = packed + ref[...]
    packed = packed / coordinates
    groups = [packed]
    for g in range(1, vectors // 8):
        groups.append(pltpu.roll(packed, LANES - vectors * g, 1))
    gram = jnp.concatenate(groups, axis=0)
    row = lax.broadcasted_iota(jnp.int32, gram.shape, 0)
    lane = lax.broadcasted_iota(jnp.int32, gram.shape, 1)
    a = jnp.where(lane < vectors, gram, jnp.where(lane == row + vectors, 1.0, 0.0))
    for panel in range(0, vectors, PANEL):
        columns = [
            jnp.broadcast_to(a[:, j : j + 1], a.shape) for j in range(panel, panel + PANEL)
        ]
        for q in range(PANEL):
            j = panel + q
            pivot = columns[q][j : j + 1, :]
            inverse = pl.reciprocal(pivot, approx=True)
            for _ in range(2):
                inverse = inverse * (2.0 - pivot * inverse)
            factor = columns[q] * inverse
            factor = jnp.where(row > j, factor, 0.0)
            for r in range(q + 1, PANEL):
                columns[r] = columns[r] - factor * columns[r][j : j + 1, :]
            a = a - factor * a[j : j + 1, :]
    diagonal = jnp.sum(jnp.where(lane == row, a, 0.0), axis=1, keepdims=True)
    a = a * (1.0 / jnp.sqrt(diagonal))
    a = jnp.where(lane < vectors, pltpu.roll(a, LANES - vectors, 1), 0.0)
    high = a.astype(BF16).astype(F32)
    left = high + pltpu.roll(high, vectors, 1) + pltpu.roll(a - high, 2 * vectors, 1)
    left = left.astype(BF16)[:, 0 : 3 * vectors]
    for n, ref in enumerate(pieces):
        for i in range(3):
            rows, lanes = pl.ds(i * vectors, vectors), pl.ds(starts[n], ref.shape[1])
            part = ref[rows, :]
            high = part.astype(BF16)
            low = (part - high.astype(F32)).astype(BF16)
            basis_ref[rows, lanes] = dot_nn(left, jnp.concatenate([high, low, high], axis=0))
            copies.append(
                pltpu.make_async_copy(
                    basis_ref.at[rows, lanes], basis_hbm.at[rows, lanes], sems.at[n, i]
                )
            )
            copies[-1].start()
    for copy in copies:
        copy.wait()


def basis_of(grams, images, vectors, coordinates):
    rows = images[0].shape[0]
    width = sum(v.shape[1] for v in images)
    return pl.pallas_call(
        functools.partial(basis_kernel, vectors, coordinates, len(grams)),
        in_specs=in_vmem(len(grams) + len(images)),
        out_specs=[pl.BlockSpec(memory_space=pl.ANY)] * 2,
        out_shape=[jax.ShapeDtypeStruct((rows, width), F32)] * 2,
        scratch_shapes=[
            pltpu.VMEM((rows, width), F32),
            pltpu.SemaphoreType.DMA((len(images), 4)),
        ],
        compiler_params=params(),
        name="basis",
    )(*grams, *images)


def to_right(z):
    return [(2 * z + core, 2 * z + 2 + core) for core in range(2)]


def to_left(z):
    return [(2 * z + core, 2 * z - 2 + core) for core in range(2)]


def along_four(pieces, make_first, make):
    inward, middle, outward = (to_right(z) + to_left(3 - z) for z in range(3))

    def at_end(chip):
        return jnp.logical_or(chip == 0, chip == 3)

    def never(chip):
        return chip < 0

    def choose(*blocks):
        def block(chip):
            return sum(jnp.where(chip == z, d, 0) for z, d in enumerate(blocks))

        return block

    each = range(pieces)
    first = [lax.ppermute(make_first(p), "frames", inward) for p in each]
    ends, middles = [], []
    for p in each:
        out = make((), choose(2, 0, 0, 1), None, p, first[p])
        ends.append(lax.ppermute(out, "frames", inward))
        out = make(first[: p + 1], choose(0, 3, 0, 0), never, p)
        middles.append(lax.ppermute(out, "frames", middle))
    arrived = []
    for p in each:
        out = make(middles[: p + 1], choose(1, 0, 3, 2), at_end, p, ends[p])
        end = lax.ppermute(out, "frames", inward + outward)
        out = make(ends[: p + 1], choose(0, 2, 1, 0), never, p, out)
        arrived.append([end, lax.ppermute(out, "frames", middle)])
    return arrived


def along_line(line, pieces, make_first, make):
    ends = to_right(0) + to_left(line - 1)
    right = [lax.ppermute(make_first(p), "frames", ends) for p in range(pieces)]
    left = list(right)
    for step in range(2, line):

        def right_block(chip, step=step):
            return jnp.minimum(line - step + chip, line - 1)

        def left_block(chip, step=step):
            return jnp.maximum(step - line + chip, 0)

        right_pairs = [pair for z in range(step) for pair in to_right(z)]
        left_pairs = [pair for z in range(step) for pair in to_left(line - 1 - z)]
        next_right, next_left = [], []
        for p in range(pieces):
            out = make(right[: p + 1], right_block, lambda chip: chip == 0, p)
            next_right.append(lax.ppermute(out, "frames", right_pairs))
            out = make(left[: p + 1], left_block, lambda chip: chip == line - 1, p)
            next_left.append(lax.ppermute(out, "frames", left_pairs))
        right, left = next_right, next_left
    return [[right[p], left[p]] for p in range(pieces)]


def per_device(atom_devices, frame_devices, frames, mean_structure, atom_weight, subspace):
    frame_rows, _, atoms = frames.shape
    vectors = subspace.shape[0]
    frame_count = frame_rows * frame_devices
    width = atoms // frame_devices
    line = frame_devices // 2
    tiles = width // LANES
    assert line > 2 and tiles > 1 and 3 * tiles + 6 <= 3 * vectors
    cut = tiles // 2 * LANES
    spans = ((0, cut), (cut, width - cut))

    x = jnp.transpose(frames, (1, 0, 2)).reshape(3 * frame_rows, atoms)
    sub = jnp.transpose(subspace, (1, 0, 2)).reshape(3 * vectors, atoms)
    where_ = lax.axis_index("frames").astype(jnp.int32).reshape(1)

    inputs = (x, mean_structure, atom_weight.reshape(1, atoms), sub)
    local, x = moments(where_, *(pltpu.with_memory_space_constraint(v, pltpu.HBM) for v in inputs))
    atom_bits = range(atom_devices.bit_length() - 1)
    coef, proj = rotate(summed(local, "atoms", atom_devices, atom_bits), frame_rows, vectors)

    swap = [(i, i ^ 1) for i in range(frame_devices)]
    proj_other = lax.ppermute(proj, "frames", swap)

    def made(keep, first, after):
        late = lax.optimization_barrier((coef, after))[0]
        return displace(where_, x, mean_structure, late, line, keep, first)

    first_sent = made(False, True, proj)
    first_own = made(True, True, first_sent)
    firsts = (first_own, lax.ppermute(first_sent, "frames", swap))
    rest_sent = made(False, False, first_own)
    rest_sent = lax.optimization_barrier((rest_sent, firsts[1], proj_other))[0]
    rest_other = lax.ppermute(rest_sent, "frames", swap)
    scales = weights(proj, proj_other, frame_rows, vectors)

    last, kept = None, []

    def make_first(p):
        nonlocal last
        last = term(where_, scales, firsts, (), None, None, line, p, spans, vectors, width)
        return last

    def rests():
        if not kept:
            kept.append(made(True, False, last))
        return kept[0], rest_other

    def make(received, block, starts, p, after=None):
        late = scales
        if after is not None:
            late = lax.optimization_barrier((scales, after))[0]
        return term(where_, late, rests(), received, block, starts, line, p, spans, vectors, width)

    if line == 4:
        arrived = along_four(len(spans), make_first, make)
    else:
        arrived = along_line(line, len(spans), make_first, make)
    image, gram, new_mean, second = first_piece(
        where_, scales, firsts, rests(), mean_structure, arrived[0], line, spans, vectors, width,
        frame_count,
    )
    images = [image]
    image, gram = second_piece(second, gram, arrived[1], vectors, frame_count)
    images.append(image)
    gram = fold(summed(gram, "atoms", atom_devices, atom_bits))
    gram = fold(exchanged(gram, "frames", frame_devices, [0]))
    grams = summed(gram, "frames", frame_devices, range(1, frame_devices.bit_length() - 1))
    image, basis = basis_of(grams, images, vectors, 3 * atoms * atom_devices)

    def placed(value):
        return jnp.transpose(value.reshape(3, vectors, width), (1, 0, 2))

    return new_mean, placed(image), placed(basis)


def solution(mesh):
    return jax.shard_map(
        functools.partial(per_device, mesh.shape["atoms"], mesh.shape["frames"]),
        mesh=mesh,
        in_specs=(P("frames", None, "atoms"), P(None, "atoms"), P("atoms"), P(None, None, "atoms")),
        out_specs=(
            P(None, ("atoms", "frames")),
            P(None, None, ("atoms", "frames")),
            P(None, None, ("atoms", "frames")),
        ),
        check_vma=False,
    )
```

```python
import functools

import jax
import jax.numpy as jnp
from jax import lax
from jax.experimental import pallas as pl
from jax.experimental.pallas import tpu as pltpu
from jax.sharding import PartitionSpec as P

NEWTON = 8
LANES = 128
F32 = jnp.float32
BF16 = jnp.bfloat16
TILE = 256
CHUNKS = 16
PANEL = 4
VMEM_LIMIT = 24 * 1024 * 1024


def params():
    return pltpu.CompilerParams(vmem_limit_bytes=VMEM_LIMIT)


def cost(weight):
    return pl.CostEstimate(flops=weight * 10**9, bytes_accessed=1, transcendentals=0)


def in_vmem(count):
    return [pl.BlockSpec(memory_space=pltpu.VMEM)] * count


def split3(value):
    high = value.astype(BF16)
    rest = value - high.astype(F32)
    middle = rest.astype(BF16)
    low = (rest - middle.astype(F32)).astype(BF16)
    return high, middle, low


def dot_nt(a, b):
    return lax.dot_general(a, b, (((1,), (1,)), ((), ())), preferred_element_type=F32)


def dot_nn(a, b, precision=None):
    return lax.dot_general(
        a, b, (((1,), (0,)), ((), ())), preferred_element_type=F32, precision=precision
    )


def moments_kernel(
    _, x_hbm, m_hbm, w_hbm, s_hbm, out_ref, x_ref, m_ref, w_ref, s_ref, sems
):
    rows, atoms = x_ref.shape
    n = rows + 8
    spans = [(t * atoms // CHUNKS, (t + 1) * atoms // CHUNKS) for t in range(CHUNKS)]
    copies = [
        [
            pltpu.make_async_copy(m_hbm, m_ref, sems.at[0, CHUNKS]),
            pltpu.make_async_copy(w_hbm, w_ref, sems.at[1, CHUNKS]),
        ]
    ]
    for t, (begin, end) in enumerate(spans):
        lanes = pl.ds(begin, end - begin)
        copies.append(
            [
                pltpu.make_async_copy(x_hbm.at[:, lanes], x_ref.at[:, lanes], sems.at[0, t]),
                pltpu.make_async_copy(s_hbm.at[:, lanes], s_ref.at[:, lanes], sems.at[1, t]),
            ]
        )
    for group in copies:
        for copy in group:
            copy.start()
    for copy in copies[0]:
        copy.wait()
    row = lax.broadcasted_iota(jnp.int32, (8, TILE), 0)
    ones = jnp.where(row == 3, 1.0, 0.0)
    total = jnp.zeros(out_ref.shape, F32)
    for t, (begin, end) in enumerate(spans):
        for copy in copies[t + 1]:
            copy.wait()
        for start in range(begin, end, TILE):
            lanes = slice(start, start + TILE)
            left = ones
            for i in range(3):
                left = jnp.where(row == i, m_ref[i : i + 1, lanes], left)
            value = jnp.concatenate([x_ref[:, lanes], left], axis=0)
            high = value.astype(BF16)
            low = (value - high.astype(F32)).astype(BF16)
            pieces = [v.astype(F32) for v in split3(left * w_ref[:, lanes])]
            aux = jnp.concatenate(pieces + [jnp.zeros(left.shape, F32)], axis=0)
            rhs = jnp.concatenate([s_ref[:, lanes], aux.astype(BF16)], axis=0)
            sums = dot_nt(jnp.concatenate([high, low], axis=0), rhs)
            total = total + (sums[0:n] + sums[n : 2 * n])
    out_ref[...] = total


def moments(where_, x, mean, weight, sub):
    rows, atoms = x.shape
    n = rows + 8
    assert atoms % (CHUNKS * TILE) == 0
    return pl.pallas_call(
        moments_kernel,
        in_specs=[pl.BlockSpec(memory_space=pltpu.SMEM)] + [pl.BlockSpec(memory_space=pl.ANY)] * 4,
        out_specs=in_vmem(2),
        out_shape=(jax.ShapeDtypeStruct((n, LANES), F32), jax.ShapeDtypeStruct(x.shape, F32)),
        scratch_shapes=[
            pltpu.VMEM(mean.shape, F32),
            pltpu.VMEM(weight.shape, F32),
            pltpu.VMEM(sub.shape, BF16),
            pltpu.SemaphoreType.DMA((2, CHUNKS + 1)),
        ],
        compiler_params=params(),
        name="moments",
    )(where_, x, mean, weight, sub)


def rotate_kernel(frame_rows, vectors, *refs):
    parts, (coef_ref, proj_ref) = refs[:-2], refs[-2:]
    sums = parts[0][...]
    for ref in parts[1:]:
        sums = sums + ref[...]
    folded = sums + pltpu.roll(sums, LANES - 8, 1) + pltpu.roll(sums, LANES - 16, 1)
    base = 3 * vectors
    tail = 3 * frame_rows
    shape = (frame_rows, LANES)
    lane = lax.broadcasted_iota(jnp.int32, shape, 1)

    def scalar(r, c):
        return jnp.broadcast_to(folded[r : r + 1, c : c + 1], shape)

    def column(j, c):
        return jnp.broadcast_to(folded[j * frame_rows : (j + 1) * frame_rows, c : c + 1], shape)

    total = scalar(tail + 3, base + 3)
    center = [scalar(tail + 3, base + i) / total for i in range(3)]
    frame_center = [column(j, base + 3) / total for j in range(3)]
    x = [
        [column(j, base + i) / total - center[i] * frame_center[j] for j in range(3)]
        for i in range(3)
    ]
    square = sum(x[i][j] * x[i][j] for i in range(3) for j in range(3))
    norm = jnp.sqrt(square)
    x = [[x[i][j] / norm for j in range(3)] for i in range(3)]
    for _ in range(NEWTON):
        cof = [
            [
                x[(i + 1) % 3][(j + 1) % 3] * x[(i + 2) % 3][(j + 2) % 3]
                - x[(i + 1) % 3][(j + 2) % 3] * x[(i + 2) % 3][(j + 1) % 3]
                for j in range(3)
            ]
            for i in range(3)
        ]
        determ = x[0][0] * cof[0][0] + x[0][1] * cof[0][1] + x[0][2] * cof[0][2]
        inverse = 1.0 / determ
        x = [[0.5 * (x[i][j] + cof[i][j] * inverse) for j in range(3)] for i in range(3)]
    shift = [
        center[i] - (x[i][0] * frame_center[0] + x[i][1] * frame_center[1] + x[i][2] * frame_center[2])
        for i in range(3)
    ]
    for i in range(3):
        for j in range(3):
            at = (3 * i + j) * frame_rows
            coef_ref[at : at + frame_rows, :] = x[i][j]
        at = (9 + i) * frame_rows
        coef_ref[at : at + frame_rows, :] = shift[i]

    def by_group(values):
        return jnp.where(lane < vectors, values[0], jnp.where(lane < 2 * vectors, values[1], values[2]))

    y = by_group(shift) * sums[tail + 3 : tail + 4, :]
    y = y - by_group([sums[tail + i : tail + i + 1, :] for i in range(3)])
    for j in range(3):
        block = sums[j * frame_rows : (j + 1) * frame_rows, :]
        y = y + by_group([x[i][j] for i in range(3)]) * block
    y = y + pltpu.roll(y, LANES - vectors, 1) + pltpu.roll(y, LANES - 2 * vectors, 1)
    y = jnp.where(lane < vectors, y, 0.0)
    proj_ref[...] = y


def rotate(parts, frame_rows, vectors):
    return pl.pallas_call(
        functools.partial(rotate_kernel, frame_rows, vectors),
        out_shape=(
            jax.ShapeDtypeStruct((12 * frame_rows, LANES), F32),
            jax.ShapeDtypeStruct((frame_rows, LANES), F32),
        ),
        compiler_params=params(),
        name="rotate",
    )(*parts)


def first_block(chip, line):
    end = jnp.logical_or(chip == 0, chip == line - 1)
    return jnp.where(end, line - 1 - chip, chip)


def displace_kernel(keep, first, line, frame_rows, width, idx, x_ref, m_ref, coef_ref, out_ref):
    core = lax.rem(idx[0], 2)
    side = core if keep else 1 - core
    made_first = first_block(idx[0] // 2, line)

    def coef(i):
        return coef_ref[i * frame_rows : (i + 1) * frame_rows, :]

    def do_block(b, _):
        block = made_first if first else b + (b >= made_first).astype(jnp.int32)
        for start in range(0, width, LANES):
            lanes = pl.ds(pl.multiple_of((2 * block + side) * width + start, LANES), LANES)
            x = [x_ref[j * frame_rows : (j + 1) * frame_rows, lanes] for j in range(3)]
            result = []
            for i in range(3):
                value = coef(3 * i) * x[0] + coef(3 * i + 1) * x[1] + coef(3 * i + 2) * x[2]
                result.append(value + (coef(9 + i) - m_ref[i : i + 1, lanes]))
            to = pl.ds(pl.multiple_of(b * width + start, LANES), LANES)
            out_ref[:, to] = jnp.concatenate(result, axis=0).astype(BF16)
        return 0

    lax.fori_loop(0, 1 if first else line - 1, do_block, 0)


def displace(where_, x, mean, coef, line, keep, first):
    rows, atoms = x.shape
    width = atoms // (2 * line)
    out_width = width if first else (line - 1) * width
    return pl.pallas_call(
        functools.partial(displace_kernel, keep, first, line, rows // 3, width),
        in_specs=[pl.BlockSpec(memory_space=pltpu.SMEM)] + in_vmem(3),
        out_specs=pl.BlockSpec(memory_space=pltpu.VMEM),
        out_shape=jax.ShapeDtypeStruct((rows, out_width), BF16),
        compiler_params=params(),
        name="displace",
    )(where_, x, mean, coef)


def weights_kernel(frame_rows, vectors, own_ref, other_ref, c_ref, e_ref, mean_ref):
    total = jnp.sum(own_ref[...] + other_ref[...], axis=0, keepdims=True)
    mean = total / (2 * frame_rows)
    lane = lax.broadcasted_iota(jnp.int32, (frame_rows, LANES), 1)
    for source, out in ((own_ref, c_ref), (other_ref, e_ref)):
        value = jnp.where(lane < vectors, source[...] - mean, 0.0)
        blocks = [value, pltpu.roll(value, vectors, 1), pltpu.roll(value, 2 * vectors, 1)]
        blocks.append(jnp.zeros((LANES - 3 * frame_rows, LANES), F32))
        table = jnp.concatenate(blocks, axis=0).T
        out[...] = table[0 : 3 * vectors, 0 : 3 * frame_rows].astype(BF16)
    mean_ref[...] = jnp.broadcast_to(jnp.where(lane[0:1] < vectors, mean, 0.0), (8, LANES))


def weights(own, other, frame_rows, vectors):
    out = jax.ShapeDtypeStruct((3 * vectors, 3 * frame_rows), BF16)
    return pl.pallas_call(
        functools.partial(weights_kernel, frame_rows, vectors),
        in_specs=in_vmem(2),
        out_specs=in_vmem(3),
        out_shape=(out, out, jax.ShapeDtypeStruct((8, LANES), F32)),
        compiler_params=params(),
        name="weights",
    )(own, other)


def ones_rows(rows):
    row = lax.broadcasted_iota(jnp.int32, (8, rows), 0)
    column = lax.broadcasted_iota(jnp.int32, (8, rows), 1)
    inside = jnp.logical_and(column >= row * (rows // 3), column < (row + 1) * (rows // 3))
    return jnp.where(inside, 1.0, 0.0).astype(BF16)


def both(left, right, a, b):
    return dot_nn(left, a) + dot_nn(right, b)


def as_column(row, vectors):
    return jnp.broadcast_to(row, (LANES, LANES)).T[0:vectors, 0:1]


def read_slab(slab, width):
    at = 3 * width // LANES
    center = jnp.sum(slab[at : at + 3], axis=0, keepdims=True)
    total = jnp.sum(slab[at + 3 : at + 6], axis=0, keepdims=True)
    return center, total


def write_slab(slab_ref, received, sums, center, total, width):
    tiles = width // LANES
    slab_ref[...] = received
    for i in range(3):
        for tile in range(tiles):
            at = i * tiles + tile
            part = sums[i : i + 1, tile * LANES : (tile + 1) * LANES]
            slab_ref[at : at + 1, :] = received[at : at + 1, :] + part
    for i, piece in enumerate([*split3(center), *split3(total)]):
        at = 3 * tiles + i
        slab_ref[at : at + 1, :] = piece.astype(F32)


def term_kernel(block, starts, line, p, spans, vectors, width, idx, *refs):
    (c_ref, e_ref, mean_ref, a_ref, b_ref), refs = refs[0:5], list(refs[5:])
    slab_ref = refs.pop() if p == 0 else None
    out_ref = refs.pop()
    chip = idx[0] // 2
    if block is None:
        at = 0
    else:
        at = block(chip)
        at = jnp.clip(at - (at > first_block(chip, line)).astype(jnp.int32), 0, line - 2)
    offset, piece_width = spans[p]
    lanes = pl.ds(pl.multiple_of(at * width + offset, LANES), piece_width)
    value = both(c_ref[...], e_ref[...], a_ref[:, lanes], b_ref[:, lanes])
    mean = mean_ref[0:1, :]
    center, total = mean, mean
    slab = jnp.zeros((value.shape[0], LANES), F32)
    ones = ones_rows(a_ref.shape[0])
    if refs:
        slab = refs[0][:, spans[0][1] :].astype(F32)
        center, summed_means = read_slab(slab, width)
        center = jnp.where(starts(chip), mean, center)
        total = mean + summed_means
        column = as_column(mean - center, vectors)
        sums = both(ones, ones, a_ref[:, lanes], b_ref[:, lanes])
        moved = [column * sums[i : i + 1, :] for i in range(3)]
        value = value + jnp.concatenate(moved, axis=0)
        value = value + refs[p][:, 0:piece_width].astype(F32)
    out_ref[:, 0:piece_width] = value.astype(BF16)
    if p == 0:
        lanes = pl.ds(pl.multiple_of(at * width, LANES), width)
        sums = both(ones, ones, a_ref[:, lanes], b_ref[:, lanes])
        write_slab(slab_ref, slab, sums, center, total, width)
        out_ref[:, piece_width:] = slab_ref[...].astype(BF16)


def term(where_, scales, displaced, received, block, starts, line, p, spans, vectors, width):
    rows = scales[0].shape[0]
    args = (*scales, *displaced, *received)
    out_width = spans[p][1] + (LANES if p == 0 else 0)
    return pl.pallas_call(
        functools.partial(term_kernel, block, starts, line, p, spans, vectors, width),
        in_specs=[pl.BlockSpec(memory_space=pltpu.SMEM)] + in_vmem(len(args)),
        out_specs=pl.BlockSpec(memory_space=pltpu.VMEM),
        out_shape=jax.ShapeDtypeStruct((rows, out_width), BF16),
        scratch_shapes=[pltpu.VMEM((rows, LANES), F32)] if p == 0 else [],
        compiler_params=params(),
        cost_estimate=cost(1),
        name="term",
    )(where_, *args)


def inner_products(parts, vectors):
    gram = jnp.zeros((2 * vectors, LANES), F32)
    for part in parts:
        high = part.astype(BF16)
        low = (part - high.astype(F32)).astype(BF16)
        lhs = jnp.concatenate([high, low], axis=0)
        rhs = jnp.concatenate([lhs, jnp.zeros((LANES - 2 * vectors, part.shape[1]), BF16)], axis=0)
        gram = gram + dot_nt(lhs, rhs)
    gram = gram[0:vectors] + gram[vectors : 2 * vectors]
    gram = gram + pltpu.roll(gram, LANES - vectors, 1)
    lane = lax.broadcasted_iota(jnp.int32, gram.shape, 1)
    gram = jnp.where(lane < vectors, gram, 0.0)
    packed = gram[0:8]
    for g in range(1, vectors // 8):
        packed = packed + pltpu.roll(gram[8 * g : 8 * g + 8], vectors * g, 1)
    return packed


def image_kernel(line, spans, vectors, width, frame_count, idx, *refs):
    refs = list(refs)
    c_ref, e_ref, mean_ref = [refs.pop(0) for _ in range(3)]
    firsts, rests = [[refs.pop(0) for _ in range(2)] for _ in range(2)]
    old_ref = refs.pop(0)
    image_ref, gram_ref, new_mean_ref, next_ref, block_ref = refs[-5:]
    received = refs[:-5]
    chip = idx[0] // 2
    made_first = first_block(chip, line)
    at = jnp.clip(chip - (chip > made_first).astype(jnp.int32), 0, line - 2) * width
    for n in range(2):

        @pl.when(chip == made_first)
        def _(n=n):
            block_ref[n] = firsts[n][...]

        @pl.when(chip != made_first)
        def _(n=n):
            block_ref[n] = rests[n][:, pl.ds(pl.multiple_of(at, LANES), width)]

    ones = ones_rows(block_ref.shape[1])
    sums = both(ones, ones, block_ref[0], block_ref[1])
    mean = mean_ref[0:1, :]
    slabs = [ref[:, spans[0][1] :].astype(F32) for ref in received]
    centers, totals = zip(*(read_slab(slab, width) for slab in slabs))
    center = functools.reduce(jnp.add, totals, mean) / line
    columns = [as_column(v - center, vectors) for v in (mean, *centers)]
    tiles = width // LANES

    def own_part(offset, piece_width):
        lanes = slice(offset, offset + piece_width)
        value = both(c_ref[...], e_ref[...], block_ref[0, :, lanes], block_ref[1, :, lanes])
        parts = []
        for i in range(3):
            moved = []
            for tile in range(offset // LANES, (offset + piece_width) // LANES):
                part = columns[0] * sums[i : i + 1, tile * LANES : (tile + 1) * LANES]
                row = i * tiles + tile
                for column, slab in zip(columns[1:], slabs):
                    part = part + column * slab[row : row + 1, :]
                moved.append(part)
            rows = slice(i * vectors, (i + 1) * vectors)
            parts.append(value[rows] + jnp.concatenate(moved, axis=1))
        return parts

    piece_width = spans[0][1]
    parts = own_part(*spans[0])
    for i in range(3):
        rows = slice(i * vectors, (i + 1) * vectors)
        for ref in received:
            parts[i] = parts[i] + ref[rows, 0:piece_width].astype(F32)
        parts[i] = parts[i] / frame_count
        image_ref[rows, :] = parts[i]
    gram_ref[...] = inner_products(parts, vectors)
    for i, part in enumerate(own_part(*spans[1])):
        next_ref[i * vectors : (i + 1) * vectors, :] = part
    total = functools.reduce(jnp.add, slabs)
    for i in range(3):
        for tile in range(tiles):
            start = (idx[0] * tiles + tile) * LANES
            old = old_ref[i : i + 1, pl.ds(pl.multiple_of(start, LANES), LANES)]
            row = i * tiles + tile
            here = slice(tile * LANES, (tile + 1) * LANES)
            added = (total[row : row + 1, :] + sums[i : i + 1, here]) / frame_count
            new_mean_ref[i : i + 1, here] = old + added


def first_piece(where_, scales, firsts, rests, mean, received, line, spans, vectors, width, frame_count):
    rows = scales[0].shape[0]
    args = (*scales, *firsts, *rests, mean, *received)
    shapes = ((rows, spans[0][1]), (8, LANES), (3, width), (rows, spans[1][1]))
    return pl.pallas_call(
        functools.partial(image_kernel, line, spans, vectors, width, frame_count),
        in_specs=[pl.BlockSpec(memory_space=pltpu.SMEM)] + in_vmem(len(args)),
        out_specs=in_vmem(len(shapes)),
        out_shape=[jax.ShapeDtypeStruct(shape, F32) for shape in shapes],
        scratch_shapes=[pltpu.VMEM((2, firsts[0].shape[0], width), BF16)],
        compiler_params=params(),
        cost_estimate=cost(2),
        name="first_piece",
    )(where_, *args)


def finish_kernel(vectors, frame_count, own_ref, before_ref, *refs):
    received, (image_ref, gram_ref) = refs[:-2], refs[-2:]
    parts = []
    for i in range(3):
        rows = slice(i * vectors, (i + 1) * vectors)
        part = own_ref[rows, :]
        for ref in received:
            part = part + ref[rows, :].astype(F32)
        parts.append(part / frame_count)
        image_ref[rows, :] = parts[i]
    gram_ref[...] = before_ref[...] + inner_products(parts, vectors)


def second_piece(own, gram, received, vectors, frame_count):
    args = (own, gram, *received)
    return pl.pallas_call(
        functools.partial(finish_kernel, vectors, frame_count),
        in_specs=in_vmem(len(args)),
        out_specs=in_vmem(2),
        out_shape=[jax.ShapeDtypeStruct(v.shape, F32) for v in (own, gram)],
        compiler_params=params(),
        name="second_piece",
    )(*args)


def fold_kernel(*refs):
    value = refs[0][...]
    for ref in refs[1:-1]:
        value = value + ref[...]
    refs[-1][...] = value


def fold(parts):
    return pl.pallas_call(
        fold_kernel,
        in_specs=in_vmem(len(parts)),
        out_specs=pl.BlockSpec(memory_space=pltpu.VMEM),
        out_shape=jax.ShapeDtypeStruct(parts[0].shape, F32),
        compiler_params=params(),
        name="fold",
    )(*parts)


def exchanged(value, axis, size, bits):
    masks = [0]
    for bit in bits:
        masks += [mask | (1 << bit) for mask in masks]
    return [value] + [
        lax.ppermute(value, axis, [(i, i ^ mask) for i in range(size)]) for mask in masks[:0:-1]
    ]


def summed(value, axis, size, bits):
    groups = [bits[start : start + 2] for start in range(0, len(bits), 2)]
    for group in groups[:-1]:
        value = fold(exchanged(value, axis, size, group))
    return exchanged(value, axis, size, groups[-1])


def basis_kernel(vectors, coordinates, gram_count, *refs):
    grams, pieces = refs[:gram_count], refs[gram_count:-4]
    image_hbm, basis_hbm, basis_ref, sems = refs[-4:]
    copies, starts = [], [0]
    for n, ref in enumerate(pieces):
        starts.append(starts[n] + ref.shape[1])
        lanes = pl.ds(starts[n], ref.shape[1])
        copies.append(pltpu.make_async_copy(ref, image_hbm.at[:, lanes], sems.at[n, 3]))
        copies[-1].start()
    packed = grams[0][...]
    for ref in grams[1:]:
        packed = packed + ref[...]
    packed = packed / coordinates
    groups = [packed]
    for g in range(1, vectors // 8):
        groups.append(pltpu.roll(packed, LANES - vectors * g, 1))
    gram = jnp.concatenate(groups, axis=0)
    row = lax.broadcasted_iota(jnp.int32, gram.shape, 0)
    lane = lax.broadcasted_iota(jnp.int32, gram.shape, 1)
    a = jnp.where(lane < vectors, gram, jnp.where(lane == row + vectors, 1.0, 0.0))
    for panel in range(0, vectors, PANEL):
        columns = [
            jnp.broadcast_to(a[:, j : j + 1], a.shape) for j in range(panel, panel + PANEL)
        ]
        for q in range(PANEL):
            j = panel + q
            pivot = columns[q][j : j + 1, :]
            factor = columns[q] * (1.0 / pivot)
            factor = jnp.where(row > j, factor, 0.0)
            for r in range(q + 1, PANEL):
                columns[r] = columns[r] - factor * columns[r][j : j + 1, :]
            a = a - factor * a[j : j + 1, :]
    diagonal = jnp.sum(jnp.where(lane == row, a, 0.0), axis=1, keepdims=True)
    a = a * (1.0 / jnp.sqrt(diagonal))
    a = jnp.where(lane < vectors, pltpu.roll(a, LANES - vectors, 1), 0.0)
    high = a.astype(BF16).astype(F32)
    left = high + pltpu.roll(high, vectors, 1) + pltpu.roll(a - high, 2 * vectors, 1)
    left = left.astype(BF16)[:, 0 : 3 * vectors]
    for n, ref in enumerate(pieces):
        for i in range(3):
            rows, lanes = pl.ds(i * vectors, vectors), pl.ds(starts[n], ref.shape[1])
            part = ref[rows, :]
            high = part.astype(BF16)
            low = (part - high.astype(F32)).astype(BF16)
            basis_ref[rows, lanes] = dot_nn(left, jnp.concatenate([high, low, high], axis=0))
            copies.append(
                pltpu.make_async_copy(
                    basis_ref.at[rows, lanes], basis_hbm.at[rows, lanes], sems.at[n, i]
                )
            )
            copies[-1].start()
    for copy in copies:
        copy.wait()


def basis_of(grams, images, vectors, coordinates):
    rows = images[0].shape[0]
    width = sum(v.shape[1] for v in images)
    return pl.pallas_call(
        functools.partial(basis_kernel, vectors, coordinates, len(grams)),
        in_specs=in_vmem(len(grams) + len(images)),
        out_specs=[pl.BlockSpec(memory_space=pl.ANY)] * 2,
        out_shape=[jax.ShapeDtypeStruct((rows, width), F32)] * 2,
        scratch_shapes=[
            pltpu.VMEM((rows, width), F32),
            pltpu.SemaphoreType.DMA((len(images), 4)),
        ],
        compiler_params=params(),
        name="basis",
    )(*grams, *images)


def to_right(z):
    return [(2 * z + core, 2 * z + 2 + core) for core in range(2)]


def to_left(z):
    return [(2 * z + core, 2 * z - 2 + core) for core in range(2)]


def along_four(pieces, make_first, make):
    inward, middle, outward = (to_right(z) + to_left(3 - z) for z in range(3))

    def at_end(chip):
        return jnp.logical_or(chip == 0, chip == 3)

    def never(chip):
        return chip < 0

    def choose(*blocks):
        def block(chip):
            return sum(jnp.where(chip == z, d, 0) for z, d in enumerate(blocks))

        return block

    each = range(pieces)
    first = [lax.ppermute(make_first(p), "frames", inward) for p in each]
    ends, middles = [], []
    for p in each:
        out = make((), choose(2, 0, 0, 1), None, p, first[p])
        ends.append(lax.ppermute(out, "frames", inward))
        out = make(first[: p + 1], choose(0, 3, 0, 0), never, p)
        middles.append(lax.ppermute(out, "frames", middle))
    arrived = []
    for p in each:
        out = make(middles[: p + 1], choose(1, 0, 3, 2), at_end, p, ends[p])
        end = lax.ppermute(out, "frames", inward + outward)
        out = make(ends[: p + 1], choose(0, 2, 1, 0), never, p, out)
        arrived.append([end, lax.ppermute(out, "frames", middle)])
    return arrived


def along_line(line, pieces, make_first, make):
    ends = to_right(0) + to_left(line - 1)
    right = [lax.ppermute(make_first(p), "frames", ends) for p in range(pieces)]
    left = list(right)
    for step in range(2, line):

        def right_block(chip, step=step):
            return jnp.minimum(line - step + chip, line - 1)

        def left_block(chip, step=step):
            return jnp.maximum(step - line + chip, 0)

        right_pairs = [pair for z in range(step) for pair in to_right(z)]
        left_pairs = [pair for z in range(step) for pair in to_left(line - 1 - z)]
        next_right, next_left = [], []
        for p in range(pieces):
            out = make(right[: p + 1], right_block, lambda chip: chip == 0, p)
            next_right.append(lax.ppermute(out, "frames", right_pairs))
            out = make(left[: p + 1], left_block, lambda chip: chip == line - 1, p)
            next_left.append(lax.ppermute(out, "frames", left_pairs))
        right, left = next_right, next_left
    return [[right[p], left[p]] for p in range(pieces)]


def per_device(atom_devices, frame_devices, frames, mean_structure, atom_weight, subspace):
    frame_rows, _, atoms = frames.shape
    vectors = subspace.shape[0]
    frame_count = frame_rows * frame_devices
    width = atoms // frame_devices
    line = frame_devices // 2
    tiles = width // LANES
    assert line > 2 and tiles > 1 and 3 * tiles + 6 <= 3 * vectors
    cut = tiles // 2 * LANES
    spans = ((0, cut), (cut, width - cut))

    x = jnp.transpose(frames, (1, 0, 2)).reshape(3 * frame_rows, atoms)
    sub = jnp.transpose(subspace, (1, 0, 2)).reshape(3 * vectors, atoms)
    where_ = lax.axis_index("frames").astype(jnp.int32).reshape(1)

    inputs = (x, mean_structure, atom_weight.reshape(1, atoms), sub)
    local, x = moments(where_, *(pltpu.with_memory_space_constraint(v, pltpu.HBM) for v in inputs))
    atom_bits = range(atom_devices.bit_length() - 1)
    coef, proj = rotate(summed(local, "atoms", atom_devices, atom_bits), frame_rows, vectors)

    swap = [(i, i ^ 1) for i in range(frame_devices)]
    proj_other = lax.ppermute(proj, "frames", swap)

    def made(keep, first, after):
        late = lax.optimization_barrier((coef, after))[0]
        return displace(where_, x, mean_structure, late, line, keep, first)

    first_sent = made(False, True, proj)
    first_own = made(True, True, first_sent)
    firsts = (first_own, lax.ppermute(first_sent, "frames", swap))
    rest_sent = made(False, False, first_own)
    rest_sent = lax.optimization_barrier((rest_sent, firsts[1], proj_other))[0]
    rest_other = lax.ppermute(rest_sent, "frames", swap)
    scales = weights(proj, proj_other, frame_rows, vectors)

    last, kept = None, []

    def make_first(p):
        nonlocal last
        last = term(where_, scales, firsts, (), None, None, line, p, spans, vectors, width)
        return last

    def rests():
        if not kept:
            kept.append(made(True, False, last))
        return kept[0], rest_other

    def make(received, block, starts, p, after=None):
        late = scales
        if after is not None:
            late = lax.optimization_barrier((scales, after))[0]
        return term(where_, late, rests(), received, block, starts, line, p, spans, vectors, width)

    if line == 4:
        arrived = along_four(len(spans), make_first, make)
    else:
        arrived = along_line(line, len(spans), make_first, make)
    image, gram, new_mean, second = first_piece(
        where_, scales, firsts, rests(), mean_structure, arrived[0], line, spans, vectors, width,
        frame_count,
    )
    images = [image]
    image, gram = second_piece(second, gram, arrived[1], vectors, frame_count)
    images.append(image)
    gram = fold(summed(gram, "atoms", atom_devices, atom_bits))
    gram = fold(exchanged(gram, "frames", frame_devices, [0]))
    grams = summed(gram, "frames", frame_devices, range(1, frame_devices.bit_length() - 1))
    image, basis = basis_of(grams, images, vectors, 3 * atoms * atom_devices)

    def placed(value):
        return jnp.transpose(value.reshape(3, vectors, width), (1, 0, 2))

    return new_mean, placed(image), placed(basis)


def solution(mesh):
    return jax.shard_map(
        functools.partial(per_device, mesh.shape["atoms"], mesh.shape["frames"]),
        mesh=mesh,
        in_specs=(P("frames", None, "atoms"), P(None, "atoms"), P("atoms"), P(None, None, "atoms")),
        out_specs=(
            P(None, ("atoms", "frames")),
            P(None, None, ("atoms", "frames")),
            P(None, None, ("atoms", "frames")),
        ),
        check_vma=False,
    )
```

```python
import functools

import jax
import jax.numpy as jnp
from jax import lax
from jax.experimental import pallas as pl
from jax.experimental.pallas import tpu as pltpu
from jax.sharding import PartitionSpec as P

NEWTON = 8
LANES = 128
F32 = jnp.float32
BF16 = jnp.bfloat16
TILE = 256
CHUNKS = 12
PANEL = 4
VMEM_LIMIT = 24 * 1024 * 1024


def params():
    return pltpu.CompilerParams(vmem_limit_bytes=VMEM_LIMIT)


def cost(weight):
    return pl.CostEstimate(flops=weight * 10**9, bytes_accessed=1, transcendentals=0)


def in_vmem(count):
    return [pl.BlockSpec(memory_space=pltpu.VMEM)] * count


def split3(value):
    high = value.astype(BF16)
    rest = value - high.astype(F32)
    middle = rest.astype(BF16)
    low = (rest - middle.astype(F32)).astype(BF16)
    return high, middle, low


def dot_nt(a, b):
    return lax.dot_general(a, b, (((1,), (1,)), ((), ())), preferred_element_type=F32)


def dot_nn(a, b, precision=None):
    return lax.dot_general(
        a, b, (((1,), (0,)), ((), ())), preferred_element_type=F32, precision=precision
    )


def moments_kernel(
    _, x_hbm, m_hbm, w_hbm, s_hbm, out_ref, x_ref, m_ref, w_ref, s_ref, sems
):
    rows, atoms = x_ref.shape
    n = rows + 8
    spans = [(t * atoms // CHUNKS, (t + 1) * atoms // CHUNKS) for t in range(CHUNKS)]
    copies = [
        [
            pltpu.make_async_copy(m_hbm, m_ref, sems.at[0, CHUNKS]),
            pltpu.make_async_copy(w_hbm, w_ref, sems.at[1, CHUNKS]),
        ]
    ]
    for t, (begin, end) in enumerate(spans):
        lanes = pl.ds(begin, end - begin)
        copies.append(
            [
                pltpu.make_async_copy(x_hbm.at[:, lanes], x_ref.at[:, lanes], sems.at[0, t]),
                pltpu.make_async_copy(s_hbm.at[:, lanes], s_ref.at[:, lanes], sems.at[1, t]),
            ]
        )
    for group in copies:
        for copy in group:
            copy.start()
    for copy in copies[0]:
        copy.wait()
    row = lax.broadcasted_iota(jnp.int32, (8, TILE), 0)
    ones = jnp.where(row == 3, 1.0, 0.0)
    total = jnp.zeros(out_ref.shape, F32)
    for t, (begin, end) in enumerate(spans):
        for copy in copies[t + 1]:
            copy.wait()
        for start in range(begin, end, TILE):
            lanes = slice(start, start + TILE)
            left = ones
            for i in range(3):
                left = jnp.where(row == i, m_ref[i : i + 1, lanes], left)
            value = jnp.concatenate([x_ref[:, lanes], left], axis=0)
            high = value.astype(BF16)
            low = (value - high.astype(F32)).astype(BF16)
            pieces = [v.astype(F32) for v in split3(left * w_ref[:, lanes])]
            aux = jnp.concatenate(pieces + [jnp.zeros(left.shape, F32)], axis=0)
            rhs = jnp.concatenate([s_ref[:, lanes], aux.astype(BF16)], axis=0)
            sums = dot_nt(jnp.concatenate([high, low], axis=0), rhs)
            total = total + (sums[0:n] + sums[n : 2 * n])
    out_ref[...] = total


def moments(where_, x, mean, weight, sub):
    rows, atoms = x.shape
    n = rows + 8
    assert atoms % (CHUNKS * TILE) == 0
    return pl.pallas_call(
        moments_kernel,
        in_specs=[pl.BlockSpec(memory_space=pltpu.SMEM)] + [pl.BlockSpec(memory_space=pl.ANY)] * 4,
        out_specs=in_vmem(2),
        out_shape=(jax.ShapeDtypeStruct((n, LANES), F32), jax.ShapeDtypeStruct(x.shape, F32)),
        scratch_shapes=[
            pltpu.VMEM(mean.shape, F32),
            pltpu.VMEM(weight.shape, F32),
            pltpu.VMEM(sub.shape, BF16),
            pltpu.SemaphoreType.DMA((2, CHUNKS + 1)),
        ],
        compiler_params=params(),
        name="moments",
    )(where_, x, mean, weight, sub)


def rotate_kernel(frame_rows, vectors, *refs):
    parts, (coef_ref, proj_ref) = refs[:-2], refs[-2:]
    sums = parts[0][...]
    for ref in parts[1:]:
        sums = sums + ref[...]
    folded = sums + pltpu.roll(sums, LANES - 8, 1) + pltpu.roll(sums, LANES - 16, 1)
    base = 3 * vectors
    tail = 3 * frame_rows
    shape = (frame_rows, LANES)
    lane = lax.broadcasted_iota(jnp.int32, shape, 1)

    def scalar(r, c):
        return jnp.broadcast_to(folded[r : r + 1, c : c + 1], shape)

    def column(j, c):
        return jnp.broadcast_to(folded[j * frame_rows : (j + 1) * frame_rows, c : c + 1], shape)

    total = scalar(tail + 3, base + 3)
    center = [scalar(tail + 3, base + i) / total for i in range(3)]
    frame_center = [column(j, base + 3) / total for j in range(3)]
    x = [
        [column(j, base + i) / total - center[i] * frame_center[j] for j in range(3)]
        for i in range(3)
    ]
    square = sum(x[i][j] * x[i][j] for i in range(3) for j in range(3))
    norm = jnp.sqrt(square)
    x = [[x[i][j] / norm for j in range(3)] for i in range(3)]
    for _ in range(NEWTON):
        cof = [
            [
                x[(i + 1) % 3][(j + 1) % 3] * x[(i + 2) % 3][(j + 2) % 3]
                - x[(i + 1) % 3][(j + 2) % 3] * x[(i + 2) % 3][(j + 1) % 3]
                for j in range(3)
            ]
            for i in range(3)
        ]
        determ = x[0][0] * cof[0][0] + x[0][1] * cof[0][1] + x[0][2] * cof[0][2]
        inverse = 1.0 / determ
        x = [[0.5 * (x[i][j] + cof[i][j] * inverse) for j in range(3)] for i in range(3)]
    shift = [
        center[i] - (x[i][0] * frame_center[0] + x[i][1] * frame_center[1] + x[i][2] * frame_center[2])
        for i in range(3)
    ]
    for i in range(3):
        for j in range(3):
            at = (3 * i + j) * frame_rows
            coef_ref[at : at + frame_rows, :] = x[i][j]
        at = (9 + i) * frame_rows
        coef_ref[at : at + frame_rows, :] = shift[i]

    def by_group(values):
        return jnp.where(lane < vectors, values[0], jnp.where(lane < 2 * vectors, values[1], values[2]))

    y = by_group(shift) * sums[tail + 3 : tail + 4, :]
    y = y - by_group([sums[tail + i : tail + i + 1, :] for i in range(3)])
    for j in range(3):
        block = sums[j * frame_rows : (j + 1) * frame_rows, :]
        y = y + by_group([x[i][j] for i in range(3)]) * block
    y = y + pltpu.roll(y, LANES - vectors, 1) + pltpu.roll(y, LANES - 2 * vectors, 1)
    y = jnp.where(lane < vectors, y, 0.0)
    proj_ref[...] = y


def rotate(parts, frame_rows, vectors):
    return pl.pallas_call(
        functools.partial(rotate_kernel, frame_rows, vectors),
        out_shape=(
            jax.ShapeDtypeStruct((12 * frame_rows, LANES), F32),
            jax.ShapeDtypeStruct((frame_rows, LANES), F32),
        ),
        compiler_params=params(),
        name="rotate",
    )(*parts)


def first_block(chip, line):
    end = jnp.logical_or(chip == 0, chip == line - 1)
    return jnp.where(end, line - 1 - chip, chip)


def displace_kernel(keep, first, line, frame_rows, width, idx, x_ref, m_ref, coef_ref, out_ref):
    core = lax.rem(idx[0], 2)
    side = core if keep else 1 - core
    made_first = first_block(idx[0] // 2, line)

    def coef(i):
        return coef_ref[i * frame_rows : (i + 1) * frame_rows, :]

    def do_block(b, _):
        block = made_first if first else b + (b >= made_first).astype(jnp.int32)
        for start in range(0, width, LANES):
            lanes = pl.ds(pl.multiple_of((2 * block + side) * width + start, LANES), LANES)
            x = [x_ref[j * frame_rows : (j + 1) * frame_rows, lanes] for j in range(3)]
            result = []
            for i in range(3):
                value = coef(3 * i) * x[0] + coef(3 * i + 1) * x[1] + coef(3 * i + 2) * x[2]
                result.append(value + (coef(9 + i) - m_ref[i : i + 1, lanes]))
            to = pl.ds(pl.multiple_of(b * width + start, LANES), LANES)
            out_ref[:, to] = jnp.concatenate(result, axis=0).astype(BF16)
        return 0

    lax.fori_loop(0, 1 if first else line - 1, do_block, 0)


def displace(where_, x, mean, coef, line, keep, first):
    rows, atoms = x.shape
    width = atoms // (2 * line)
    out_width = width if first else (line - 1) * width
    return pl.pallas_call(
        functools.partial(displace_kernel, keep, first, line, rows // 3, width),
        in_specs=[pl.BlockSpec(memory_space=pltpu.SMEM)] + in_vmem(3),
        out_specs=pl.BlockSpec(memory_space=pltpu.VMEM),
        out_shape=jax.ShapeDtypeStruct((rows, out_width), BF16),
        compiler_params=params(),
        name="displace",
    )(where_, x, mean, coef)


def weights_kernel(frame_rows, vectors, own_ref, other_ref, c_ref, e_ref, mean_ref):
    total = jnp.sum(own_ref[...] + other_ref[...], axis=0, keepdims=True)
    mean = total / (2 * frame_rows)
    lane = lax.broadcasted_iota(jnp.int32, (frame_rows, LANES), 1)
    for source, out in ((own_ref, c_ref), (other_ref, e_ref)):
        value = jnp.where(lane < vectors, source[...] - mean, 0.0)
        blocks = [value, pltpu.roll(value, vectors, 1), pltpu.roll(value, 2 * vectors, 1)]
        blocks.append(jnp.zeros((LANES - 3 * frame_rows, LANES), F32))
        table = jnp.concatenate(blocks, axis=0).T
        out[...] = table[0 : 3 * vectors, 0 : 3 * frame_rows].astype(BF16)
    mean_ref[...] = jnp.broadcast_to(jnp.where(lane[0:1] < vectors, mean, 0.0), (8, LANES))


def weights(own, other, frame_rows, vectors):
    out = jax.ShapeDtypeStruct((3 * vectors, 3 * frame_rows), BF16)
    return pl.pallas_call(
        functools.partial(weights_kernel, frame_rows, vectors),
        in_specs=in_vmem(2),
        out_specs=in_vmem(3),
        out_shape=(out, out, jax.ShapeDtypeStruct((8, LANES), F32)),
        compiler_params=params(),
        name="weights",
    )(own, other)


def ones_rows(rows):
    row = lax.broadcasted_iota(jnp.int32, (8, rows), 0)
    column = lax.broadcasted_iota(jnp.int32, (8, rows), 1)
    inside = jnp.logical_and(column >= row * (rows // 3), column < (row + 1) * (rows // 3))
    return jnp.where(inside, 1.0, 0.0).astype(BF16)


def both(left, right, a, b):
    return dot_nn(left, a) + dot_nn(right, b)


def as_column(row, vectors):
    return jnp.broadcast_to(row, (LANES, LANES)).T[0:vectors, 0:1]


def read_slab(slab, width):
    at = 3 * width // LANES
    center = jnp.sum(slab[at : at + 3], axis=0, keepdims=True)
    total = jnp.sum(slab[at + 3 : at + 6], axis=0, keepdims=True)
    return center, total


def write_slab(slab_ref, received, sums, center, total, width):
    tiles = width // LANES
    slab_ref[...] = received
    for i in range(3):
        for tile in range(tiles):
            at = i * tiles + tile
            part = sums[i : i + 1, tile * LANES : (tile + 1) * LANES]
            slab_ref[at : at + 1, :] = received[at : at + 1, :] + part
    for i, piece in enumerate([*split3(center), *split3(total)]):
        at = 3 * tiles + i
        slab_ref[at : at + 1, :] = piece.astype(F32)


def term_kernel(block, starts, line, p, spans, vectors, width, idx, *refs):
    (c_ref, e_ref, mean_ref, a_ref, b_ref), refs = refs[0:5], list(refs[5:])
    slab_ref = refs.pop() if p == 0 else None
    out_ref = refs.pop()
    chip = idx[0] // 2
    if block is None:
        at = 0
    else:
        at = block(chip)
        at = jnp.clip(at - (at > first_block(chip, line)).astype(jnp.int32), 0, line - 2)
    offset, piece_width = spans[p]
    lanes = pl.ds(pl.multiple_of(at * width + offset, LANES), piece_width)
    value = both(c_ref[...], e_ref[...], a_ref[:, lanes], b_ref[:, lanes])
    mean = mean_ref[0:1, :]
    center, total = mean, mean
    slab = jnp.zeros((value.shape[0], LANES), F32)
    ones = ones_rows(a_ref.shape[0])
    if refs:
        slab = refs[0][:, spans[0][1] :].astype(F32)
        center, summed_means = read_slab(slab, width)
        center = jnp.where(starts(chip), mean, center)
        total = mean + summed_means
        column = as_column(mean - center, vectors)
        sums = both(ones, ones, a_ref[:, lanes], b_ref[:, lanes])
        moved = [column * sums[i : i + 1, :] for i in range(3)]
        value = value + jnp.concatenate(moved, axis=0)
        value = value + refs[p][:, 0:piece_width].astype(F32)
    out_ref[:, 0:piece_width] = value.astype(BF16)
    if p == 0:
        lanes = pl.ds(pl.multiple_of(at * width, LANES), width)
        sums = both(ones, ones, a_ref[:, lanes], b_ref[:, lanes])
        write_slab(slab_ref, slab, sums, center, total, width)
        out_ref[:, piece_width:] = slab_ref[...].astype(BF16)


def term(where_, scales, displaced, received, block, starts, line, p, spans, vectors, width):
    rows = scales[0].shape[0]
    args = (*scales, *displaced, *received)
    out_width = spans[p][1] + (LANES if p == 0 else 0)
    return pl.pallas_call(
        functools.partial(term_kernel, block, starts, line, p, spans, vectors, width),
        in_specs=[pl.BlockSpec(memory_space=pltpu.SMEM)] + in_vmem(len(args)),
        out_specs=pl.BlockSpec(memory_space=pltpu.VMEM),
        out_shape=jax.ShapeDtypeStruct((rows, out_width), BF16),
        scratch_shapes=[pltpu.VMEM((rows, LANES), F32)] if p == 0 else [],
        compiler_params=params(),
        cost_estimate=cost(1),
        name="term",
    )(where_, *args)


def inner_products(parts, vectors):
    gram = jnp.zeros((2 * vectors, LANES), F32)
    for part in parts:
        high = part.astype(BF16)
        low = (part - high.astype(F32)).astype(BF16)
        lhs = jnp.concatenate([high, low], axis=0)
        rhs = jnp.concatenate([lhs, jnp.zeros((LANES - 2 * vectors, part.shape[1]), BF16)], axis=0)
        gram = gram + dot_nt(lhs, rhs)
    gram = gram[0:vectors] + gram[vectors : 2 * vectors]
    gram = gram + pltpu.roll(gram, LANES - vectors, 1)
    lane = lax.broadcasted_iota(jnp.int32, gram.shape, 1)
    gram = jnp.where(lane < vectors, gram, 0.0)
    packed = gram[0:8]
    for g in range(1, vectors // 8):
        packed = packed + pltpu.roll(gram[8 * g : 8 * g + 8], vectors * g, 1)
    return packed


def image_kernel(line, spans, vectors, width, frame_count, idx, *refs):
    refs = list(refs)
    c_ref, e_ref, mean_ref = [refs.pop(0) for _ in range(3)]
    firsts, rests = [[refs.pop(0) for _ in range(2)] for _ in range(2)]
    old_ref = refs.pop(0)
    image_ref, gram_ref, new_mean_ref, next_ref, block_ref = refs[-5:]
    received = refs[:-5]
    chip = idx[0] // 2
    made_first = first_block(chip, line)
    at = jnp.clip(chip - (chip > made_first).astype(jnp.int32), 0, line - 2) * width
    for n in range(2):

        @pl.when(chip == made_first)
        def _(n=n):
            block_ref[n] = firsts[n][...]

        @pl.when(chip != made_first)
        def _(n=n):
            block_ref[n] = rests[n][:, pl.ds(pl.multiple_of(at, LANES), width)]

    ones = ones_rows(block_ref.shape[1])
    sums = both(ones, ones, block_ref[0], block_ref[1])
    mean = mean_ref[0:1, :]
    slabs = [ref[:, spans[0][1] :].astype(F32) for ref in received]
    centers, totals = zip(*(read_slab(slab, width) for slab in slabs))
    center = functools.reduce(jnp.add, totals, mean) / line
    columns = [as_column(v - center, vectors) for v in (mean, *centers)]
    tiles = width // LANES

    def own_part(offset, piece_width):
        lanes = slice(offset, offset + piece_width)
        value = both(c_ref[...], e_ref[...], block_ref[0, :, lanes], block_ref[1, :, lanes])
        parts = []
        for i in range(3):
            moved = []
            for tile in range(offset // LANES, (offset + piece_width) // LANES):
                part = columns[0] * sums[i : i + 1, tile * LANES : (tile + 1) * LANES]
                row = i * tiles + tile
                for column, slab in zip(columns[1:], slabs):
                    part = part + column * slab[row : row + 1, :]
                moved.append(part)
            rows = slice(i * vectors, (i + 1) * vectors)
            parts.append(value[rows] + jnp.concatenate(moved, axis=1))
        return parts

    piece_width = spans[0][1]
    parts = own_part(*spans[0])
    for i in range(3):
        rows = slice(i * vectors, (i + 1) * vectors)
        for ref in received:
            parts[i] = parts[i] + ref[rows, 0:piece_width].astype(F32)
        parts[i] = parts[i] / frame_count
        image_ref[rows, :] = parts[i]
    gram_ref[...] = inner_products(parts, vectors)
    for i, part in enumerate(own_part(*spans[1])):
        next_ref[i * vectors : (i + 1) * vectors, :] = part
    total = functools.reduce(jnp.add, slabs)
    for i in range(3):
        for tile in range(tiles):
            start = (idx[0] * tiles + tile) * LANES
            old = old_ref[i : i + 1, pl.ds(pl.multiple_of(start, LANES), LANES)]
            row = i * tiles + tile
            here = slice(tile * LANES, (tile + 1) * LANES)
            added = (total[row : row + 1, :] + sums[i : i + 1, here]) / frame_count
            new_mean_ref[i : i + 1, here] = old + added


def first_piece(where_, scales, firsts, rests, mean, received, line, spans, vectors, width, frame_count):
    rows = scales[0].shape[0]
    args = (*scales, *firsts, *rests, mean, *received)
    shapes = ((rows, spans[0][1]), (8, LANES), (3, width), (rows, spans[1][1]))
    return pl.pallas_call(
        functools.partial(image_kernel, line, spans, vectors, width, frame_count),
        in_specs=[pl.BlockSpec(memory_space=pltpu.SMEM)] + in_vmem(len(args)),
        out_specs=in_vmem(len(shapes)),
        out_shape=[jax.ShapeDtypeStruct(shape, F32) for shape in shapes],
        scratch_shapes=[pltpu.VMEM((2, firsts[0].shape[0], width), BF16)],
        compiler_params=params(),
        cost_estimate=cost(2),
        name="first_piece",
    )(where_, *args)


def finish_kernel(vectors, frame_count, own_ref, before_ref, *refs):
    received, (image_ref, gram_ref) = refs[:-2], refs[-2:]
    parts = []
    for i in range(3):
        rows = slice(i * vectors, (i + 1) * vectors)
        part = own_ref[rows, :]
        for ref in received:
            part = part + ref[rows, :].astype(F32)
        parts.append(part / frame_count)
        image_ref[rows, :] = parts[i]
    gram_ref[...] = before_ref[...] + inner_products(parts, vectors)


def second_piece(own, gram, received, vectors, frame_count):
    args = (own, gram, *received)
    return pl.pallas_call(
        functools.partial(finish_kernel, vectors, frame_count),
        in_specs=in_vmem(len(args)),
        out_specs=in_vmem(2),
        out_shape=[jax.ShapeDtypeStruct(v.shape, F32) for v in (own, gram)],
        compiler_params=params(),
        name="second_piece",
    )(*args)


def fold_kernel(*refs):
    value = refs[0][...]
    for ref in refs[1:-1]:
        value = value + ref[...]
    refs[-1][...] = value


def fold(parts):
    return pl.pallas_call(
        fold_kernel,
        in_specs=in_vmem(len(parts)),
        out_specs=pl.BlockSpec(memory_space=pltpu.VMEM),
        out_shape=jax.ShapeDtypeStruct(parts[0].shape, F32),
        compiler_params=params(),
        name="fold",
    )(*parts)


def exchanged(value, axis, size, bits):
    masks = [0]
    for bit in bits:
        masks += [mask | (1 << bit) for mask in masks]
    return [value] + [
        lax.ppermute(value, axis, [(i, i ^ mask) for i in range(size)]) for mask in masks[:0:-1]
    ]


def summed(value, axis, size, bits):
    groups = [bits[start : start + 2] for start in range(0, len(bits), 2)]
    for group in groups[:-1]:
        value = fold(exchanged(value, axis, size, group))
    return exchanged(value, axis, size, groups[-1])


def basis_kernel(vectors, coordinates, gram_count, *refs):
    grams, pieces = refs[:gram_count], refs[gram_count:-4]
    image_hbm, basis_hbm, basis_ref, sems = refs[-4:]
    copies, starts = [], [0]
    for n, ref in enumerate(pieces):
        starts.append(starts[n] + ref.shape[1])
        lanes = pl.ds(starts[n], ref.shape[1])
        copies.append(pltpu.make_async_copy(ref, image_hbm.at[:, lanes], sems.at[n, 3]))
        copies[-1].start()
    packed = grams[0][...]
    for ref in grams[1:]:
        packed = packed + ref[...]
    packed = packed / coordinates
    groups = [packed]
    for g in range(1, vectors // 8):
        groups.append(pltpu.roll(packed, LANES - vectors * g, 1))
    gram = jnp.concatenate(groups, axis=0)
    row = lax.broadcasted_iota(jnp.int32, gram.shape, 0)
    lane = lax.broadcasted_iota(jnp.int32, gram.shape, 1)
    a = jnp.where(lane < vectors, gram, jnp.where(lane == row + vectors, 1.0, 0.0))
    for panel in range(0, vectors, PANEL):
        columns = [
            jnp.broadcast_to(a[:, j : j + 1], a.shape) for j in range(panel, panel + PANEL)
        ]
        for q in range(PANEL):
            j = panel + q
            pivot = columns[q][j : j + 1, :]
            factor = columns[q] * (1.0 / pivot)
            factor = jnp.where(row > j, factor, 0.0)
            for r in range(q + 1, PANEL):
                columns[r] = columns[r] - factor * columns[r][j : j + 1, :]
            a = a - factor * a[j : j + 1, :]
    diagonal = jnp.sum(jnp.where(lane == row, a, 0.0), axis=1, keepdims=True)
    a = a * (1.0 / jnp.sqrt(diagonal))
    a = jnp.where(lane < vectors, pltpu.roll(a, LANES - vectors, 1), 0.0)
    high = a.astype(BF16).astype(F32)
    left = high + pltpu.roll(high, vectors, 1) + pltpu.roll(a - high, 2 * vectors, 1)
    left = left.astype(BF16)[:, 0 : 3 * vectors]
    for n, ref in enumerate(pieces):
        for i in range(3):
            rows, lanes = pl.ds(i * vectors, vectors), pl.ds(starts[n], ref.shape[1])
            part = ref[rows, :]
            high = part.astype(BF16)
            low = (part - high.astype(F32)).astype(BF16)
            basis_ref[rows, lanes] = dot_nn(left, jnp.concatenate([high, low, high], axis=0))
            copies.append(
                pltpu.make_async_copy(
                    basis_ref.at[rows, lanes], basis_hbm.at[rows, lanes], sems.at[n, i]
                )
            )
            copies[-1].start()
    for copy in copies:
        copy.wait()


def basis_of(grams, images, vectors, coordinates):
    rows = images[0].shape[0]
    width = sum(v.shape[1] for v in images)
    return pl.pallas_call(
        functools.partial(basis_kernel, vectors, coordinates, len(grams)),
        in_specs=in_vmem(len(grams) + len(images)),
        out_specs=[pl.BlockSpec(memory_space=pl.ANY)] * 2,
        out_shape=[jax.ShapeDtypeStruct((rows, width), F32)] * 2,
        scratch_shapes=[
            pltpu.VMEM((rows, width), F32),
            pltpu.SemaphoreType.DMA((len(images), 4)),
        ],
        compiler_params=params(),
        name="basis",
    )(*grams, *images)


def to_right(z):
    return [(2 * z + core, 2 * z + 2 + core) for core in range(2)]


def to_left(z):
    return [(2 * z + core, 2 * z - 2 + core) for core in range(2)]


def along_four(pieces, make_first, make):
    inward, middle, outward = (to_right(z) + to_left(3 - z) for z in range(3))

    def at_end(chip):
        return jnp.logical_or(chip == 0, chip == 3)

    def never(chip):
        return chip < 0

    def choose(*blocks):
        def block(chip):
            return sum(jnp.where(chip == z, d, 0) for z, d in enumerate(blocks))

        return block

    each = range(pieces)
    first = [lax.ppermute(make_first(p), "frames", inward) for p in each]
    ends, middles = [], []
    for p in each:
        out = make((), choose(2, 0, 0, 1), None, p, first[p])
        ends.append(lax.ppermute(out, "frames", inward))
        out = make(first[: p + 1], choose(0, 3, 0, 0), never, p)
        middles.append(lax.ppermute(out, "frames", middle))
    arrived = []
    for p in each:
        out = make(middles[: p + 1], choose(1, 0, 3, 2), at_end, p, ends[p])
        end = lax.ppermute(out, "frames", inward + outward)
        out = make(ends[: p + 1], choose(0, 2, 1, 0), never, p, out)
        arrived.append([end, lax.ppermute(out, "frames", middle)])
    return arrived


def along_line(line, pieces, make_first, make):
    ends = to_right(0) + to_left(line - 1)
    right = [lax.ppermute(make_first(p), "frames", ends) for p in range(pieces)]
    left = list(right)
    for step in range(2, line):

        def right_block(chip, step=step):
            return jnp.minimum(line - step + chip, line - 1)

        def left_block(chip, step=step):
            return jnp.maximum(step - line + chip, 0)

        right_pairs = [pair for z in range(step) for pair in to_right(z)]
        left_pairs = [pair for z in range(step) for pair in to_left(line - 1 - z)]
        next_right, next_left = [], []
        for p in range(pieces):
            out = make(right[: p + 1], right_block, lambda chip: chip == 0, p)
            next_right.append(lax.ppermute(out, "frames", right_pairs))
            out = make(left[: p + 1], left_block, lambda chip: chip == line - 1, p)
            next_left.append(lax.ppermute(out, "frames", left_pairs))
        right, left = next_right, next_left
    return [[right[p], left[p]] for p in range(pieces)]


def per_device(atom_devices, frame_devices, frames, mean_structure, atom_weight, subspace):
    frame_rows, _, atoms = frames.shape
    vectors = subspace.shape[0]
    frame_count = frame_rows * frame_devices
    width = atoms // frame_devices
    line = frame_devices // 2
    tiles = width // LANES
    assert line > 2 and tiles > 1 and 3 * tiles + 6 <= 3 * vectors
    cut = tiles // 2 * LANES
    spans = ((0, cut), (cut, width - cut))

    x = jnp.transpose(frames, (1, 0, 2)).reshape(3 * frame_rows, atoms)
    sub = jnp.transpose(subspace, (1, 0, 2)).reshape(3 * vectors, atoms)
    where_ = lax.axis_index("frames").astype(jnp.int32).reshape(1)

    inputs = (x, mean_structure, atom_weight.reshape(1, atoms), sub)
    local, x = moments(where_, *(pltpu.with_memory_space_constraint(v, pltpu.HBM) for v in inputs))
    atom_bits = range(atom_devices.bit_length() - 1)
    coef, proj = rotate(summed(local, "atoms", atom_devices, atom_bits), frame_rows, vectors)

    swap = [(i, i ^ 1) for i in range(frame_devices)]
    proj_other = lax.ppermute(proj, "frames", swap)

    def made(keep, first, after):
        late = lax.optimization_barrier((coef, after))[0]
        return displace(where_, x, mean_structure, late, line, keep, first)

    first_sent = made(False, True, proj)
    first_own = made(True, True, first_sent)
    firsts = (first_own, lax.ppermute(first_sent, "frames", swap))
    rest_sent = made(False, False, first_own)
    rest_sent = lax.optimization_barrier((rest_sent, firsts[1], proj_other))[0]
    rest_other = lax.ppermute(rest_sent, "frames", swap)
    scales = weights(proj, proj_other, frame_rows, vectors)

    last, kept = None, []

    def make_first(p):
        nonlocal last
        last = term(where_, scales, firsts, (), None, None, line, p, spans, vectors, width)
        return last

    def rests():
        if not kept:
            kept.append(made(True, False, last))
        return kept[0], rest_other

    def make(received, block, starts, p, after=None):
        late = scales
        if after is not None:
            late = lax.optimization_barrier((scales, after))[0]
        return term(where_, late, rests(), received, block, starts, line, p, spans, vectors, width)

    if line == 4:
        arrived = along_four(len(spans), make_first, make)
    else:
        arrived = along_line(line, len(spans), make_first, make)
    image, gram, new_mean, second = first_piece(
        where_, scales, firsts, rests(), mean_structure, arrived[0], line, spans, vectors, width,
        frame_count,
    )
    images = [image]
    image, gram = second_piece(second, gram, arrived[1], vectors, frame_count)
    images.append(image)
    gram = fold(summed(gram, "atoms", atom_devices, atom_bits))
    gram = fold(exchanged(gram, "frames", frame_devices, [0]))
    grams = summed(gram, "frames", frame_devices, range(1, frame_devices.bit_length() - 1))
    image, basis = basis_of(grams, images, vectors, 3 * atoms * atom_devices)

    def placed(value):
        return jnp.transpose(value.reshape(3, vectors, width), (1, 0, 2))

    return new_mean, placed(image), placed(basis)


def solution(mesh):
    return jax.shard_map(
        functools.partial(per_device, mesh.shape["atoms"], mesh.shape["frames"]),
        mesh=mesh,
        in_specs=(P("frames", None, "atoms"), P(None, "atoms"), P("atoms"), P(None, None, "atoms")),
        out_specs=(
            P(None, ("atoms", "frames")),
            P(None, None, ("atoms", "frames")),
            P(None, None, ("atoms", "frames")),
        ),
        check_vma=False,
    )
```
